128 devices in a mesh: dp: 32 (over z, y, core), proto: 4 (over x).
Axes of the slice: x: 4, y: 4, z: 4, core: 2. Of those that a mesh axis runs over, the one named last changes fastest.
Arguments:
- teacher_feat: bfloat16 [65536, 256], P('dp'), may hold values from -100 to 100
- student_feat: bfloat16 [65536, 256], P('dp'), may hold values from -100 to 100
- teacher_proto: bfloat16 [256, 65536], P('dp', 'proto'), may hold values from -1.6 to 1.6
- student_proto: bfloat16 [256, 65536], P('dp', 'proto'), may hold values from -1.6 to 1.6
- mask_index: int32 [12288], P('dp'), may hold values from 0 to 2047, as said below
- mask_count: int32 [32], P('dp'), may hold values from 192 to 384, as said below
Outputs:
- token_loss: float32 [12288], P('dp')
- proto_grad: float32 [256, 65536], P('dp', 'proto')
The draws below stay inside these ranges and needn't reach their ends.
Inputs may be any that keep to these rules, and one draw needn't show every extreme that they name: `mask_index`: within one index of dp the 384 slots name distinct patch tokens of its 2048; slots at or past its count hold indices too and are ignored. `mask_count`: some index of dp has all 384 slots live in every draw.
All inputs are finite; a program needn't handle non-finite values.
Results may differ from the reference program's by a relative error of at most 0.003.
Values may be sent and summed in bfloat16 or wider, within the bound.
No kernel may reach another device: no remote copies, remote signals or barrier semaphores. Data moves between devices by JAX's collectives and lax.ppermute only.
A program may use at most 192 MiB of HBM per device.

```python
import math
import jax
import jax.numpy as jnp
from jax import lax

D_BOT = 256
PROTOS = 65536
PATCH = 256
SWEEPS = 3
IMG_DEV = 8
MASK_DEV = 384
IMAGES = 256
PATCHES = 65536
N_DP = 32


def shared_layout(seed_key):
    center_key, block_key, label_key = jax.random.split(seed_key, 3)
    centers = jax.random.truncated_normal(center_key, -6.0, 6.0, (64, D_BOT), jnp.float32) * D_BOT ** (-0.5)
    block_cluster = (jax.random.permutation(block_key, 256) // 4).astype(jnp.int32)
    column_block = jnp.arange(PROTOS, dtype=jnp.int32) * 256 // PROTOS
    column_cluster = block_cluster[column_block]
    token_cluster = jax.random.randint(label_key, (PATCHES,), 0, 64, jnp.int32)
    return (centers, column_cluster, token_cluster)


def feature_rows(seed_key, centers, token_cluster):
    first_key = jax.random.fold_in(seed_key, 0)
    fourth_key = jax.random.fold_in(seed_key, 3)
    normal_part = jax.random.truncated_normal(first_key, -6.0, 6.0, (PATCHES, D_BOT), jnp.float32)
    row_scale = jnp.exp(jax.random.uniform(fourth_key, (PATCHES, 1), jnp.float32, 0.0, math.log(10.0)))
    noise = normal_part
    aligned = 0.8 * D_BOT ** 0.5 * centers[token_cluster] + 0.6 * noise
    return jnp.clip(aligned * row_scale, -100.0, 100.0).astype(jnp.bfloat16)


def proto_columns_draw(seed_key, centers, column_cluster):
    first_key = jax.random.fold_in(seed_key, 0)
    third_key = jax.random.fold_in(seed_key, 2)
    normal_part = jax.random.truncated_normal(first_key, -6.0, 6.0, (D_BOT, PROTOS), jnp.float32)
    col_scale = jnp.exp(jax.random.uniform(third_key, (1, PROTOS), jnp.float32, math.log(0.3), math.log(3.0)))
    noise = normal_part * D_BOT ** (-0.5)
    aligned = 0.8 * centers[column_cluster].T + 0.6 * noise
    return jnp.clip(aligned * col_scale, -1.6, 1.6).astype(jnp.bfloat16)


def draw_teacher_feat(key, part):
    centers, column_cluster, token_cluster = shared_layout(key)
    key = jax.random.fold_in(key, 11)
    return feature_rows(key, centers, token_cluster)


def draw_student_feat(key, part):
    centers, column_cluster, token_cluster = shared_layout(key)
    key = jax.random.fold_in(key, 13)
    return feature_rows(key, centers, token_cluster)


def draw_teacher_proto(key, part):
    centers, column_cluster, token_cluster = shared_layout(key)
    key = jax.random.fold_in(key, 17)
    return proto_columns_draw(key, centers, column_cluster)


def draw_student_proto(key, part):
    centers, column_cluster, token_cluster = shared_layout(key)
    key = jax.random.fold_in(key, 19)
    return proto_columns_draw(key, centers, column_cluster)


def draw_mask_index(key, part):
    key = jax.random.fold_in(key, 31)
    group_keys = jax.random.split(key, N_DP)
    picked = jax.vmap(lambda group_key: jax.random.permutation(group_key, IMG_DEV * PATCH)[:MASK_DEV])(group_keys)
    return picked.astype(jnp.int32).reshape(-1)


def draw_mask_count(key, part):
    key = jax.random.fold_in(key, 37)
    first_key, second_key = jax.random.split(key, 2)
    counts = jax.random.randint(first_key, (N_DP,), MASK_DEV // 2, MASK_DEV + 1, jnp.int32)
    filled = jax.random.randint(second_key, (), 0, N_DP, jnp.int32)
    return jnp.where(jnp.arange(N_DP, dtype=jnp.int32) == filled, MASK_DEV, counts).astype(jnp.int32)


def setup_inputs(seed: int = 0) -> dict:
    keys = jax.random.split(jax.random.key(seed), 7)
    return {
        "teacher_feat": draw_teacher_feat(jax.random.fold_in(keys[6], 71), 0),
        "student_feat": draw_student_feat(jax.random.fold_in(keys[6], 71), 0),
        "teacher_proto": draw_teacher_proto(jax.random.fold_in(keys[6], 71), 0),
        "student_proto": draw_student_proto(jax.random.fold_in(keys[6], 71), 0),
        "mask_index": draw_mask_index(jax.random.fold_in(keys[6], 71), 0),
        "mask_count": draw_mask_count(jax.random.fold_in(keys[6], 71), 0),
    }


teacher_temp = 0.07
student_temp = 0.1
loss_scale = 65536.0
precise = lax.Precision.HIGHEST

def token_setup(mask_index, mask_count):
    slot_ids = jnp.arange(N_DP * MASK_DEV, dtype=jnp.int32)
    group_of = slot_ids // MASK_DEV
    live_rows = (slot_ids % MASK_DEV < mask_count[group_of]).astype(jnp.float32)
    image_of = mask_index // PATCH
    onehot = (image_of.reshape(N_DP, MASK_DEV, 1) == jnp.arange(IMG_DEV, dtype=jnp.int32)).astype(jnp.float32)
    per_image = lax.optimization_barrier(jnp.sum(onehot * live_rows.reshape(N_DP, MASK_DEV, 1), axis=1))
    own_count = lax.optimization_barrier(jnp.sum(onehot * per_image[:, None, :], axis=2)).reshape(-1)
    token_weight = live_rows / (jnp.maximum(own_count, 1.0) * IMAGES)
    source_rows = (mask_index + group_of * (IMG_DEV * PATCH)).astype(jnp.int32)
    return (live_rows, token_weight, source_rows)

def unit_rows(features):
    wide = features.astype(jnp.float32)
    return (wide * lax.rsqrt(lax.optimization_barrier(jnp.sum(wide * wide, axis=1, keepdims=True)) + 1e-06)).astype(jnp.bfloat16)

def column_scale(proto):
    wide = proto.astype(jnp.float32)
    return lax.rsqrt(lax.optimization_barrier(jnp.sum(wide * wide, axis=0)) + 1e-06)

def reference(teacher_feat, student_feat, teacher_proto, student_proto, mask_index, mask_count):
    live_rows, token_weight, source_rows = token_setup(mask_index, mask_count)
    teacher_unit = unit_rows(teacher_feat[source_rows])
    student_unit = unit_rows(student_feat[source_rows])
    inv_t = column_scale(teacher_proto)
    inv_s = column_scale(student_proto)
    energy = jnp.exp(jnp.dot(teacher_unit, teacher_proto, preferred_element_type=jnp.float32) * inv_t / teacher_temp)
    scale_r = live_rows
    scale_c = jnp.zeros((PROTOS,), jnp.float32)
    for sweep_no in range(SWEEPS):
        scale_c = 1.0 / jnp.dot(scale_r, energy, precision=precise)
        if sweep_no + 1 < SWEEPS:
            scale_r = live_rows / jnp.dot(energy, scale_c, precision=precise)
    block_rows = math.gcd(N_DP * MASK_DEV, 512)
    block_count = N_DP * MASK_DEV // block_rows

    def block_step(totals, block_no):
        grad_acc, dot_acc = totals
        offset = (block_no * block_rows).astype(jnp.int32)
        energy_blk = lax.dynamic_slice_in_dim(energy, offset, block_rows, 0)
        unit_blk = lax.dynamic_slice_in_dim(student_unit, offset, block_rows, 0)
        live_blk = lax.dynamic_slice_in_dim(live_rows, offset, block_rows, 0)
        weight_blk = lax.dynamic_slice_in_dim(token_weight, offset, block_rows, 0)
        cosine = jnp.dot(unit_blk, student_proto, preferred_element_type=jnp.float32) * inv_s
        logits = cosine / student_temp
        exp_terms = jnp.exp(logits)
        weighted = energy_blk * scale_c
        row_mass = jnp.dot(energy_blk, scale_c, precision=precise)
        cross_mass = lax.optimization_barrier(jnp.sum(weighted * logits, axis=1))
        softmax_sum = lax.optimization_barrier(jnp.sum(exp_terms, axis=1))
        loss_blk = live_blk * (jnp.log(softmax_sum) - cross_mass / row_mass)
        target = weighted / row_mass[:, None]
        grad_bf = (loss_scale * weight_blk[:, None] * (exp_terms / softmax_sum[:, None] - target) / student_temp).astype(jnp.bfloat16)
        dot_acc = dot_acc + lax.optimization_barrier(jnp.sum(grad_bf.astype(jnp.float32) * cosine, axis=0))
        grad_acc = grad_acc + jnp.dot(unit_blk.T, grad_bf, preferred_element_type=jnp.float32)
        return ((grad_acc, dot_acc), loss_blk)
    init = (jnp.zeros((D_BOT, PROTOS), jnp.float32), jnp.zeros((PROTOS,), jnp.float32))
    (grad_unit, column_dot), losses = lax.scan(block_step, init, jnp.arange(block_count, dtype=jnp.int32))
    token_loss = losses.reshape(-1)
    proto_grad = inv_s * (grad_unit - student_proto.astype(jnp.float32) * inv_s * column_dot)
    return (token_loss, proto_grad)
```

```python
import functools

import jax
import jax.numpy as jnp
from jax import lax
from jax.experimental import pallas as pl
from jax.experimental.pallas import tpu as pltpu
from jax.sharding import PartitionSpec as P

PATCH = 256
EXTRA = 16
LOG2E = 1.4426950408889634

teacher_temp = 0.07
student_temp = 0.1
loss_scale = 65536.0

f32 = jnp.float32
bf16 = jnp.bfloat16


def params(mib):
    return pltpu.CompilerParams(vmem_limit_bytes=mib * 1024 * 1024)


def nn(a, b):
    return lax.dot_general(a, b, (((1,), (0,)), ((), ())), preferred_element_type=f32)


def nt(a, b):
    return lax.dot_general(a, b, (((1,), (1,)), ((), ())), preferred_element_type=f32)


def tokens_kernel(count_ref, index_ref, teacher_ref, student_ref, t_out, s_out):
    slots = index_ref.shape[1]
    source = teacher_ref.shape[0]
    index_row = index_ref[...]
    index_col = jnp.transpose(jnp.broadcast_to(index_row, (8, slots)))[:, 0:1]
    count = count_ref[0]
    live_row = lax.broadcasted_iota(jnp.int32, (1, slots), 1) < count
    live_col = lax.broadcasted_iota(jnp.int32, (slots, 1), 0) < count
    same = ((index_col >> 8) == (index_row >> 8)) & live_col
    own = jnp.sum(jnp.where(same, 1.0, 0.0), axis=0, keepdims=True)
    own = jnp.where(live_row, own, 0.0)
    pick = jnp.where(
        lax.broadcasted_iota(jnp.int32, (slots, source), 1) == index_col, 1.0, 0.0
    ).astype(bf16)
    for src, dst in ((teacher_ref, t_out), (student_ref, s_out)):
        rows = nn(pick, src[...])
        unit = rows * lax.rsqrt(jnp.sum(rows * rows, axis=1, keepdims=True) + 1e-06)
        dst[0 : unit.shape[1], :] = jnp.transpose(unit).astype(bf16)
    d = teacher_ref.shape[1]
    t_out[d : d + EXTRA, :] = jnp.broadcast_to(own, (EXTRA, slots)).astype(bf16)


def tokens(count, index, teacher_feat, student_feat):
    slots, d = index.shape[0], teacher_feat.shape[1]
    vm = pl.BlockSpec(memory_space=pltpu.VMEM)
    return pl.pallas_call(
        tokens_kernel,
        out_shape=(
            jax.ShapeDtypeStruct((d + EXTRA, slots), bf16),
            jax.ShapeDtypeStruct((d, slots), bf16),
        ),
        in_specs=[pl.BlockSpec(memory_space=pltpu.SMEM), vm, vm, vm],
        out_specs=(vm, vm),
        compiler_params=params(32),
        name="token_rows",
    )(count, index.reshape(1, slots), teacher_feat, student_feat)


def column_scale(wide_t):
    return lax.rsqrt(jnp.sum(wide_t * wide_t, axis=1, keepdims=True) + 1e-06)


def pair(ref):
    return jnp.concatenate([ref[0], ref[1]], axis=1)


def fold(m):
    total = m[:, 0:128]
    for k in range(1, m.shape[1] // 128):
        total = total + m[:, 128 * k : 128 * (k + 1)]
    return total


def energy_kernel(u_ref, w_ref, e_ref, row_ref, own_ref, wt, scale, acc, e_all, own_all):
    step, steps = pl.program_id(0), pl.num_programs(0)
    d = w_ref.shape[0]

    @pl.when(step == 0)
    def _():
        wide = jnp.transpose(w_ref[...].astype(f32))
        wt[...] = wide.astype(bf16)
        scale[...] = column_scale(wide) * (LOG2E / teacher_temp)
        acc[...] = jnp.zeros_like(acc)

    block = pair(u_ref)
    own = block[d : d + 8, :].astype(f32)[0:1, :]
    own_ref[0] = own
    live = jnp.where(own > 0.0, 1.0, 0.0)
    width = block.shape[1]
    for k in range(0, width, 256):
        raw = nn(wt[...], block[0:d, k : k + 256])
        energy = jnp.exp2(raw * scale[...])
        acc[...] += fold(energy * live[:, k : k + 256])
        low = energy.astype(bf16)
        e_ref[0, :, k : k + 256] = low
        e_all[step, :, k : k + 256] = low

    @pl.when(step == steps - 1)
    def _():
        c = 1.0 / jnp.sum(acc[...], axis=1, keepdims=True)

        def rows(i, _):
            row_ref[i] = jnp.sum(e_all[i].astype(f32) * c, axis=0, keepdims=True)
            return 0

        lax.fori_loop(0, e_all.shape[0], rows, 0)


def energy_pass(blocks, w):
    groups, rows, slots = blocks.shape
    d, cols = w.shape
    steps, width = groups // 2, 2 * slots
    return pl.pallas_call(
        energy_kernel,
        grid=(steps,),
        out_shape=(
            jax.ShapeDtypeStruct((steps, cols, width), bf16),
            jax.ShapeDtypeStruct((steps, 1, width), f32),
            jax.ShapeDtypeStruct((steps, 1, width), f32),
        ),
        in_specs=[
            pl.BlockSpec((2, rows, slots), lambda i: (i, 0, 0)),
            pl.BlockSpec((d, cols), lambda i: (0, 0)),
        ],
        out_specs=(
            pl.BlockSpec((1, cols, width), lambda i: (i, 0, 0)),
            pl.BlockSpec((steps, 1, width), lambda i: (0, 0, 0)),
            pl.BlockSpec((1, 1, width), lambda i: (i, 0, 0)),
        ),
        scratch_shapes=[
            pltpu.VMEM((cols, d), bf16),
            pltpu.VMEM((cols, 1), f32),
            pltpu.VMEM((cols, 128), f32),
            pltpu.VMEM((steps, cols, width), bf16),
            pltpu.VMEM((steps, 1, width), f32),
        ],
        compiler_params=params(48),
        name="energy_pass",
    )(blocks, w)


def load_all(hbm, vmem, sems):
    copies = [
        pltpu.make_async_copy(hbm.at[i], vmem.at[i], sems.at[i]) for i in range(vmem.shape[0])
    ]
    return copies


def column_pass(e_all, own_ref, total_ref, acc):
    acc[...] = jnp.zeros_like(acc)

    def cols(i, _):
        r = jnp.where(own_ref[i] > 0.0, 1.0, 0.0) / total_ref[i]
        acc[...] += fold(e_all[i].astype(f32) * r)
        return 0

    return cols


def sweep_kernel(own_ref, total_ref, e_ref, row_ref, acc, e_all, sems):
    steps = e_all.shape[0]

    def copy(i):
        return pltpu.make_async_copy(e_ref.at[i], e_all.at[i], sems.at[i])

    lax.fori_loop(0, steps, lambda i, _: (copy(i).start(), 0)[1], 0)
    body = column_pass(e_all, own_ref, total_ref, acc)

    def cols(i, _):
        copy(i).wait()
        return body(i, 0)

    lax.fori_loop(0, steps, cols, 0)
    c = 1.0 / jnp.sum(acc[...], axis=1, keepdims=True)

    def rows(i, _):
        row_ref[i] = jnp.sum(e_all[i].astype(f32) * c, axis=0, keepdims=True)
        return 0

    lax.fori_loop(0, steps, rows, 0)


def sweep_pass(own, total, energy):
    steps, cols, width = energy.shape
    vm = pl.BlockSpec(memory_space=pltpu.VMEM)
    return pl.pallas_call(
        sweep_kernel,
        out_shape=jax.ShapeDtypeStruct((steps, 1, width), f32),
        in_specs=[vm, vm, pl.BlockSpec(memory_space=pl.ANY)],
        out_specs=vm,
        scratch_shapes=[
            pltpu.VMEM((cols, 128), f32),
            pltpu.VMEM((steps, cols, width), bf16),
            pltpu.SemaphoreType.DMA((steps,)),
        ],
        compiler_params=params(48),
        name="sweep_pass",
    )(own, total, energy)


def softmax_kernel(u_ref, w_ref, sum_ref, wt, scale):
    @pl.when(pl.program_id(0) == 0)
    def _():
        wide = jnp.transpose(w_ref[...].astype(f32))
        wt[...] = wide.astype(bf16)
        scale[...] = column_scale(wide) * (LOG2E / student_temp)

    block = pair(u_ref)
    for k in range(0, block.shape[1], 256):
        raw = nn(wt[...], block[:, k : k + 256])
        sum_ref[0, :, k : k + 256] = jnp.sum(
            jnp.exp2(raw * scale[...]), axis=0, keepdims=True
        )


def softmax_pass(blocks, w):
    groups, d, slots = blocks.shape
    cols = w.shape[1]
    steps, width = groups // 2, 2 * slots
    return pl.pallas_call(
        softmax_kernel,
        grid=(steps,),
        out_shape=jax.ShapeDtypeStruct((steps, 1, width), f32),
        in_specs=[
            pl.BlockSpec((2, d, slots), lambda i: (i, 0, 0)),
            pl.BlockSpec((d, cols), lambda i: (0, 0)),
        ],
        out_specs=pl.BlockSpec((1, 1, width), lambda i: (i, 0, 0)),
        scratch_shapes=[pltpu.VMEM((cols, d), bf16), pltpu.VMEM((cols, 1), f32)],
        compiler_params=params(32),
        name="softmax_pass",
    )(blocks, w)


def closing_kernel(own_ref, total_ref, e_ref, u_ref, w_ref, c_ref, mass_ref, cross_ref,
                   acc, e_all, u_all, wt, sems, u_sems):
    steps = e_all.shape[0]

    def copy(i):
        return pltpu.make_async_copy(e_ref.at[i], e_all.at[i], sems.at[i])

    def copy_u(i):
        return pltpu.make_async_copy(
            u_ref.at[pl.ds(2 * i, 2)], u_all.at[pl.ds(2 * i, 2)], u_sems.at[i]
        )

    lax.fori_loop(0, steps, lambda i, _: (copy(i).start(), 0)[1], 0)
    lax.fori_loop(0, steps, lambda i, _: (copy_u(i).start(), 0)[1], 0)
    wide = jnp.transpose(w_ref[...].astype(f32))
    wt[...] = wide.astype(bf16)
    body = column_pass(e_all, own_ref, total_ref, acc)

    def cols(i, _):
        copy(i).wait()
        return body(i, 0)

    lax.fori_loop(0, steps, cols, 0)
    c = 1.0 / jnp.sum(acc[...], axis=1, keepdims=True)
    c_ref[...] = c
    cs = c * (column_scale(wide) * (1.0 / student_temp))

    def rows(i, _):
        copy_u(i).wait()
        block = pair(u_all.at[pl.ds(2 * i, 2)])
        for k in range(0, block.shape[1], 256):
            raw = nn(wt[...], block[:, k : k + 256])
            energy = e_all[i, :, k : k + 256].astype(f32)
            mass_ref[i, :, k : k + 256] = jnp.sum(energy * c, axis=0, keepdims=True)
            cross_ref[i, :, k : k + 256] = jnp.sum(
                energy * cs * raw, axis=0, keepdims=True
            )
        return 0

    lax.fori_loop(0, steps, rows, 0)


def closing_pass(own, total, energy, blocks, w):
    steps, cols, width = energy.shape
    d = w.shape[0]
    vm = pl.BlockSpec(memory_space=pltpu.VMEM)
    hbm = pl.BlockSpec(memory_space=pl.ANY)
    return pl.pallas_call(
        closing_kernel,
        out_shape=(
            jax.ShapeDtypeStruct((cols, 1), f32),
            jax.ShapeDtypeStruct((steps, 1, width), f32),
            jax.ShapeDtypeStruct((steps, 1, width), f32),
        ),
        in_specs=[vm, vm, hbm, hbm, vm],
        out_specs=(vm, vm, vm),
        scratch_shapes=[
            pltpu.VMEM((cols, 128), f32),
            pltpu.VMEM((steps, cols, width), bf16),
            pltpu.VMEM(blocks.shape, bf16),
            pltpu.VMEM((cols, d), bf16),
            pltpu.SemaphoreType.DMA((steps,)),
            pltpu.SemaphoreType.DMA((steps,)),
        ],
        compiler_params=params(48),
        name="closing_pass",
    )(own, total, energy, blocks, w)


def grad_kernel(images, own_ref, mass_ref, soft_ref, e_ref, u_ref, w_ref, c_ref, g_ref,
                wt, scale, acc):
    step = pl.program_id(0)

    @pl.when(step == 0)
    def _():
        wide = jnp.transpose(w_ref[...].astype(f32))
        wt[...] = wide.astype(bf16)
        scale[...] = column_scale(wide) * (LOG2E / student_temp)
        acc[...] = jnp.zeros_like(acc)

    block = pair(u_ref)
    own = own_ref[0]
    weight = jnp.where(own > 0.0, 1.0, 0.0) / (jnp.maximum(own, 1.0) * images)
    weight = weight * (loss_scale / student_temp)
    soft_w = weight / soft_ref[0]
    mass_w = weight / mass_ref[0]
    for k in range(0, block.shape[1], 256):
        part = block[:, k : k + 256]
        raw = nn(wt[...], part)
        soft = jnp.exp2(raw * scale[...]) * soft_w[:, k : k + 256]
        target = e_ref[0, :, k : k + 256].astype(f32) * c_ref[...] * mass_w[:, k : k + 256]
        acc[...] += nt((soft - target).astype(bf16), part)

    @pl.when(step == pl.num_programs(0) - 1)
    def _():
        wide = jnp.transpose(w_ref[...].astype(f32))
        inv = column_scale(wide)
        grad = acc[...]
        unit = wide * inv
        dot = jnp.sum(grad * unit, axis=1, keepdims=True)
        g_ref[...] = jnp.transpose(inv * (grad - unit * dot))


def grad_pass(images, own, mass, soft, energy, blocks, w, c):
    steps, cols, width = energy.shape
    d, slots = blocks.shape[1:]
    vec = pl.BlockSpec((1, 1, width), lambda i: (i, 0, 0))
    return pl.pallas_call(
        functools.partial(grad_kernel, float(images)),
        grid=(steps,),
        out_shape=jax.ShapeDtypeStruct((d, cols), f32),
        in_specs=[
            vec,
            vec,
            vec,
            pl.BlockSpec((1, cols, width), lambda i: (i, 0, 0)),
            pl.BlockSpec((2, d, slots), lambda i: (i, 0, 0)),
            pl.BlockSpec((d, cols), lambda i: (0, 0)),
            pl.BlockSpec((cols, 1), lambda i: (0, 0)),
        ],
        out_specs=pl.BlockSpec((d, cols), lambda i: (0, 0)),
        scratch_shapes=[
            pltpu.VMEM((cols, d), bf16),
            pltpu.VMEM((cols, 1), f32),
            pltpu.VMEM((cols, d), f32),
        ],
        compiler_params=params(32),
        name="grad_pass",
    )(own, mass, soft, energy, blocks, w, c)


def dp_shift(value, part, k):
    size, stride = {"z": (4, 8), "y": (4, 2), "core": (2, 1)}[part]
    perm = []
    for i in range(32):
        at = (i // stride) % size
        perm.append((i, i + (((at + k) % size) - at) * stride))
    return lax.ppermute(value, "dp", perm)


def x_shift(value, k):
    return lax.ppermute(value, "proto", [(i, (i + k) % 4) for i in range(4)])


def total_of(value):
    value = value + dp_shift(value, "core", 1)
    value = value + x_shift(value, 1) + x_shift(value, 3) + x_shift(value, 2)
    for part in ("y", "z"):
        value = (
            value
            + dp_shift(value, part, 1)
            + dp_shift(value, part, 3)
            + dp_shift(value, part, 2)
        )
    return value


def local(teacher_feat, student_feat, teacher_proto, student_proto, mask_index, mask_count):
    slots = mask_index.shape[0]
    groups = lax.axis_size("dp")
    images = groups * (teacher_feat.shape[0] // PATCH)
    t_block, s_block = tokens(mask_count, mask_index, teacher_feat, student_feat)
    t_blocks = lax.all_gather(t_block, "dp", axis=0)
    s_blocks = lax.all_gather(s_block, "dp", axis=0)
    t_w = lax.all_to_all(teacher_proto, "dp", 1, 0, tiled=True)
    s_w = lax.all_to_all(student_proto, "dp", 1, 0, tiled=True)
    energy, row, own = energy_pass(t_blocks, t_w)
    total = total_of(row)
    soft_part = softmax_pass(s_blocks, s_w)
    row = sweep_pass(own, total, energy)
    both = total_of(jnp.concatenate([row, soft_part], axis=1))
    total, soft = both[:, 0:1], both[:, 1:2]
    c, mass_part, cross_part = closing_pass(own, total, energy, s_blocks, s_w)
    mass = total_of(mass_part)
    cross = total_of(cross_part)
    grad = grad_pass(images, own, mass, soft, energy, s_blocks, s_w, c)
    proto_grad = lax.all_to_all(grad, "dp", 0, 1, tiled=True)
    start = lax.axis_index("dp") * slots

    def mine(v):
        return lax.dynamic_slice_in_dim(v.reshape(-1), start, slots, 0)

    live = (jnp.arange(slots, dtype=jnp.int32) < mask_count[0]).astype(f32)
    token_loss = live * (jnp.log(mine(soft)) - mine(cross) / mine(mass))
    return (token_loss, proto_grad)


def solution(mesh):
    return jax.shard_map(
        local,
        mesh=mesh,
        in_specs=(
            P("dp", None),
            P("dp", None),
            P("dp", "proto"),
            P("dp", "proto"),
            P("dp"),
            P("dp"),
        ),
        out_specs=(P("dp"), P("dp", "proto")),
        check_vma=False,
    )
```

```python
import functools

import jax
import jax.numpy as jnp
from jax import lax
from jax.experimental import pallas as pl
from jax.experimental.pallas import tpu as pltpu
from jax.sharding import Mesh
from jax.sharding import PartitionSpec as P

PATCH = 256
SWEEPS = 3
EXTRA = 16
LOG2E = 1.4426950408889634
ROWS = 64
SURE = 192
WIDE = 256
PER = 3
TALL = 32
LANES = 128
SHIFTS = (1, 3, 2)
SIDE = 4
GROUP = ("z", "c", "x")

teacher_temp = 0.07
student_temp = 0.1
loss_scale = 65536.0

f32 = jnp.float32
bf16 = jnp.bfloat16

VM = pl.BlockSpec(memory_space=pltpu.VMEM)
SM = pl.BlockSpec(memory_space=pltpu.SMEM)
ANY = pl.BlockSpec(memory_space=pl.ANY)


def params(mib):
    return pltpu.CompilerParams(vmem_limit_bytes=mib * 1024 * 1024)


def pinned(array):
    return pltpu.with_memory_space_constraint(array, pltpu.VMEM)


def shape(dims, dtype=f32):
    return jax.ShapeDtypeStruct(dims, dtype)


def nn(a, b):
    return lax.dot_general(a, b, (((1,), (0,)), ((), ())), preferred_element_type=f32)


def tn(a, b):
    return lax.dot_general(a, b, (((0,), (0,)), ((), ())), preferred_element_type=f32)


def tokens_kernel(me_ref, count_ref, index_ref, teacher_ref, student_ref, tp_ref, sp_ref,
                  t_out, s_out, w_out, info_out, feats, protos, sems, p_sems):
    proto_copies = [
        pltpu.make_async_copy(ref, protos.at[i], p_sems.at[i])
        for i, ref in enumerate((tp_ref, sp_ref))
    ]
    copies = [
        pltpu.make_async_copy(ref, feats.at[i], sems.at[i])
        for i, ref in enumerate((teacher_ref, student_ref))
    ]
    for c in proto_copies + copies:
        c.start()
    me = me_ref[0]
    z, y, core = me >> 3, (me >> 1) & 3, me & 1
    info_out[0] = z
    info_out[1] = core
    slots = index_ref.shape[0]
    source, d = feats.shape[1:]
    index_row = index_ref[...].reshape(1, slots)
    index_col = jnp.transpose(jnp.broadcast_to(index_row, (8, slots)))[:, 0:1]
    count = count_ref[0]
    live_row = lax.broadcasted_iota(jnp.int32, (1, slots), 1) < count
    live_col = lax.broadcasted_iota(jnp.int32, (slots, 1), 0) < count
    same = ((index_col >> 8) == (index_row >> 8)) & live_col
    own = jnp.sum(jnp.where(same, 1.0, 0.0), axis=0, keepdims=True)
    own = jnp.where(live_row, own, 0.0)
    rest = jnp.concatenate([own[:, d:], jnp.zeros((1, 2 * d - slots), f32)], axis=1)
    at = lax.broadcasted_iota(jnp.int32, (EXTRA, d), 0)
    counts = jnp.where(at == 0, own[:, 0:d], jnp.where(at == 1, rest, 0.0))
    t_out[slots : slots + EXTRA, :] = counts.astype(bf16)
    pick = jnp.where(
        lax.broadcasted_iota(jnp.int32, (slots, source), 1) == index_col, 1.0, 0.0
    ).astype(bf16)
    to = lax.broadcasted_iota(jnp.int32, (1, d), 1)
    turn = to >> 6
    shift = jnp.where(turn == 2, 3, jnp.where(turn == 3, 2, turn))
    origin = (
        ((to >> 4) & 3) * 64 + ((y + 4 - shift) & 3) * 16 + ((to >> 3) & 1) * 8 + (to & 7)
    )
    order = jnp.where(
        lax.broadcasted_iota(jnp.int32, (d, d), 0) == origin, 1.0, 0.0
    ).astype(bf16)
    for c in proto_copies:
        c.wait()
    parts, _, width = w_out.shape
    for q in range(parts):
        lanes = slice(q * width, (q + 1) * width)
        w_out[q] = jnp.concatenate(
            [protos[0, :, lanes].astype(f32), protos[1, :, lanes].astype(f32)], axis=0
        ).astype(bf16)
    for i, out in enumerate((t_out, s_out)):
        copies[i].wait()
        rows = nn(pick, feats[i])
        unit = rows * lax.rsqrt(jnp.sum(rows * rows, axis=1, keepdims=True) + 1e-06)
        out[0:slots, :] = nn(unit.astype(bf16), order).astype(bf16)


def tokens(me, count, index, teacher_feat, student_feat, teacher_proto, student_proto):
    slots, (source, d) = index.shape[0], teacher_feat.shape
    rows, cols = teacher_proto.shape
    parts = 8
    return pl.pallas_call(
        tokens_kernel,
        out_shape=(
            shape((slots + EXTRA, d), bf16),
            shape((slots, d), bf16),
            shape((parts, 2 * rows, cols // parts), bf16),
            shape((2,), jnp.int32),
        ),
        in_specs=[SM, SM, VM, ANY, ANY, ANY, ANY],
        out_specs=(VM, VM, VM, SM),
        scratch_shapes=[
            pltpu.VMEM((2, source, d), bf16),
            pltpu.VMEM((2, rows, cols), bf16),
            pltpu.SemaphoreType.DMA((2,)),
            pltpu.SemaphoreType.DMA((2,)),
        ],
        compiler_params=params(56),
        name="token_rows",
    )(me, count, index, teacher_feat, student_feat, teacher_proto, student_proto)


def split_kernel(which, w_ref, tok_ref, *refs):
    out, tok_out = refs[-2:]
    parts, rows, width = w_ref.shape
    out[...] = (
        w_ref[...].astype(f32)[:, 8 * which : 8 * which + 8]
        .reshape(parts * 8, width)
        .astype(bf16)
    )
    tok_out[...] = tok_ref[...]


def split(which, w, tok, after=()):
    parts, rows, width = w.shape
    return pl.pallas_call(
        functools.partial(split_kernel, which),
        out_shape=(shape((parts * rows // 2, width), bf16), shape(tok.shape, bf16)),
        in_specs=[VM, VM] + [ANY] * len(after),
        out_specs=(VM, VM),
        compiler_params=params(16),
        name="split_rows",
    )(w, tok, *after)


def token_copies(info_ref, refs, dst, sems):
    z, core = info_ref[0], info_ref[1]
    copies = []
    for a, ref in enumerate(refs):
        k = (0,) + SHIFTS
        at = ((z + 4 - k[a % 4]) & 3) * 2 + (core if a < 4 else 1 - core)
        copies.append(
            pltpu.make_async_copy(ref, dst.at[at], sems.at[a])
        )
    return copies


def weight_copies(refs, dst, sems):
    rows = refs[0].shape[0]
    return [
        pltpu.make_async_copy(ref, dst.at[pl.ds(i * rows, rows)], sems.at[i])
        for i, ref in enumerate(refs)
    ]


def inverse_norms(w_ref):
    wide = w_ref[...].astype(f32)
    return lax.rsqrt(jnp.sum(wide * wide, axis=0, keepdims=True) + 1e-06)


def down(rows):
    return jnp.concatenate(
        [
            jnp.transpose(jnp.broadcast_to(rows[j : j + 1, :], (LANES, LANES)))
            for j in range(rows.shape[0])
        ],
        axis=0,
    )


def across(parts_ref):
    return jnp.concatenate(
        [
            jnp.sum(jnp.transpose(parts_ref[j : j + LANES, :]), axis=0, keepdims=True)
            for j in range(0, parts_ref.shape[0], LANES)
        ],
        axis=0,
    )


def vector(ref, b, first=0):
    return ref[pl.ds(first + PER * b, PER), :]


def added(parts_ref):
    total = parts_ref[0].astype(f32)
    for i in range(1, parts_ref.shape[0]):
        total = total + parts_ref[i].astype(f32)
    return total


def live_of(own):
    return jnp.where(own > 0.0, 1.0, 0.0)


def column_factor(refs):
    total = refs[0][...]
    for ref in refs[1:]:
        total = total + ref[...]
    return 1.0 / total


def chunks(n, size):
    return [slice(at, at + size) for at in range(0, n, size)]


def energy_kernel(info_ref, *refs):
    toks, w_refs = refs[0:8], refs[8:12]
    e_ref, own_ref, sum_ref, u, w, live, acc, t_sems, w_sems = refs[-9:]
    blocks, slots, cols = e_ref.shape
    t_copies = token_copies(info_ref, toks, u, t_sems)
    w_copies = weight_copies(w_refs, w, w_sems)
    for c in t_copies + w_copies:
        c.start()
    for c in w_copies:
        c.wait()
    scale = inverse_norms(w) * (LOG2E / teacher_temp)
    acc[...] = jnp.zeros_like(acc)
    own_ref[...] = jnp.zeros_like(own_ref)
    for c in t_copies:
        c.wait()

    def step(b, _):
        counts = u[b, slots : slots + EXTRA, :].astype(f32)
        for j in range(PER):
            row, lane = divmod(j * LANES, counts.shape[1])
            own_ref[pl.ds(PER * b + j, 1), :] = counts[row : row + 1, lane : lane + LANES]
        live[...] = down(live_of(vector(own_ref, b)))
        for n in chunks(cols, WIDE):
            raw = nn(u[b, 0:slots, :], w[:, n])
            for i in range(0, WIDE, LANES):
                k = slice(n.start + i, n.start + i + LANES)
                total = acc[:, k]
                for r in chunks(slots, ROWS):
                    energy = jnp.exp2(raw[r, i : i + LANES] * scale[:, k])
                    e_ref[b, r, k] = energy.astype(bf16)
                    total = total + (energy * live[r, :] if r.stop > SURE else energy)
                acc[:, k] = total
        return 0

    lax.fori_loop(0, blocks, step, 0)
    sum_ref[...] = jnp.sum(acc[...], axis=0, keepdims=True)


def energy_pass(info, toks, w_parts, slots, after):
    d, cols = SIDE * w_parts[0].shape[0], w_parts[0].shape[1]
    blocks = len(toks)
    return pl.pallas_call(
        energy_kernel,
        out_shape=(
            pltpu.VMEM((blocks, slots, cols), bf16),
            shape((TALL, LANES)),
            shape((1, cols)),
        ),
        in_specs=[SM] + [ANY] * (blocks + len(w_parts) + len(after)),
        out_specs=(VM, VM, VM),
        scratch_shapes=[
            pltpu.VMEM((blocks, slots + EXTRA, d), bf16),
            pltpu.VMEM((d, cols), bf16),
            pltpu.VMEM((slots, LANES), f32),
            pltpu.VMEM((ROWS, cols), f32),
            pltpu.SemaphoreType.DMA((blocks,)),
            pltpu.SemaphoreType.DMA((len(w_parts),)),
        ],
        compiler_params=params(16),
        cost_estimate=pl.CostEstimate(
            flops=2 * blocks * slots * cols * d,
            transcendentals=blocks * slots * cols,
            bytes_accessed=2 * blocks * slots * cols,
        ),
        name="energy_pass",
    )(info, *toks, *w_parts, *after)


def row_kernel(*refs):
    sums, (e, *_, out_ref, part, rows) = refs[0:SIDE], refs[SIDE:]
    blocks, slots, cols = e.shape
    c = column_factor(sums)
    rows[...] = jnp.zeros_like(rows)

    def step(b, _):
        for r in chunks(slots, ROWS):
            total = jnp.zeros((ROWS, LANES), f32)
            for k in chunks(cols, LANES):
                total = total + e[b, r, k].astype(f32) * c[:, k]
            part[r, :] = total
        rows[pl.ds(PER * b, PER), :] = across(part)
        return 0

    lax.fori_loop(0, blocks, step, 0)
    low = rows[...].astype(bf16)
    for i in range(out_ref.shape[0]):
        out_ref[i] = low


def row_pass(sums, energy, peers, after=()):
    blocks, slots, cols = energy.shape
    return pl.pallas_call(
        row_kernel,
        out_shape=shape((peers, TALL, LANES), bf16),
        in_specs=[VM] * (SIDE + 1) + [ANY] * len(after),
        out_specs=VM,
        scratch_shapes=[
            pltpu.VMEM((slots, LANES), f32),
            pltpu.VMEM((TALL, LANES), f32),
        ],
        compiler_params=params(8),
        name="row_pass",
    )(*sums, pinned(energy), *after)


def column_kernel(rows_ref, own_ref, e, out_ref, weight, ratio, acc):
    blocks, slots, cols = e.shape
    acc[...] = jnp.zeros_like(acc)
    own = own_ref[...]
    ratio[...] = live_of(own) / jnp.where(own > 0.0, added(rows_ref), 1.0)

    def step(b, _):
        weight[...] = down(vector(ratio, b))
        for k in chunks(cols, LANES):
            total = acc[:, k]
            for r in chunks(slots, ROWS):
                total = total + e[b, r, k].astype(f32) * weight[r, :]
            acc[:, k] = total
        return 0

    lax.fori_loop(0, blocks, step, 0)
    out_ref[...] = jnp.sum(acc[...], axis=0, keepdims=True)


def column_pass(rows, own, energy):
    blocks, slots, cols = energy.shape
    return pl.pallas_call(
        column_kernel,
        out_shape=shape((1, cols)),
        in_specs=[VM, VM, VM],
        out_specs=VM,
        scratch_shapes=[
            pltpu.VMEM((slots, LANES), f32),
            pltpu.VMEM((TALL, LANES), f32),
            pltpu.VMEM((ROWS, cols), f32),
        ],
        compiler_params=params(8),
        name="column_pass",
    )(rows, own, pinned(energy))


def closing_kernel(info_ref, *refs):
    toks, w_refs, sums = refs[0:8], refs[8:12], refs[12 : 12 + SIDE]
    e, u, ut, w, out_ref, part, rows, crosses, t_sems, w_sems = refs[12 + SIDE :]
    blocks, slots, cols = e.shape
    t_copies = token_copies(info_ref, toks, u, t_sems)
    w_copies = weight_copies(w_refs, w, w_sems)
    for copy in w_copies + t_copies:
        copy.start()
    c = column_factor(sums)
    for copy in w_copies + t_copies:
        copy.wait()
    scale = inverse_norms(w) * (LOG2E / student_temp)
    rows[...] = jnp.zeros_like(rows)

    def step(b, _):
        ut[b] = jnp.transpose(u[b].astype(f32)).astype(bf16)
        for tall in chunks(slots, LANES):
            raw = nn(u[b, tall, :], w[...])
            for at in chunks(LANES, ROWS):
                r = slice(tall.start + at.start, tall.start + at.stop)
                mass = jnp.zeros((ROWS, LANES), f32)
                cross = jnp.zeros((ROWS, LANES), f32)
                total = jnp.zeros((ROWS, LANES), f32)
                for k in chunks(cols, LANES):
                    power = raw[at, k] * scale[:, k]
                    total = total + jnp.exp2(power)
                    energy = e[b, r, k].astype(f32) * c[:, k]
                    mass = mass + energy
                    cross = cross + energy * power
                part[0, r, :] = mass
                part[1, r, :] = total
                part[2, r, :] = cross
        rows[pl.ds(PER * b, PER), :] = across(part.at[0])
        rows[pl.ds(PER * (blocks + b), PER), :] = across(part.at[1])
        crosses[b, 0:PER, :] = across(part.at[2]) * (1.0 / LOG2E)
        return 0

    lax.fori_loop(0, blocks, step, 0)
    at = 2 * PER * blocks
    for i in range(out_ref.shape[0]):
        rows[at : at + PER, :] = crosses[i // 4, 0:PER, :]
        out_ref[i] = rows[...].astype(bf16)


def closing_pass(info, toks, w_parts, sums, energy, peers):
    blocks, slots, cols = energy.shape
    d = SIDE * w_parts[0].shape[0]
    return pl.pallas_call(
        closing_kernel,
        out_shape=(
            pltpu.VMEM((blocks, slots, d), bf16),
            pltpu.VMEM((blocks, d, slots), bf16),
            pltpu.VMEM((d, cols), bf16),
            shape((peers, 2 * TALL, LANES), bf16),
        ),
        in_specs=[SM] + [ANY] * (blocks + len(w_parts)) + [VM] * (SIDE + 1),
        out_specs=(VM, VM, VM, VM),
        scratch_shapes=[
            pltpu.VMEM((3, slots, LANES), f32),
            pltpu.VMEM((2 * TALL, LANES), f32),
            pltpu.VMEM((blocks, 8, LANES), f32),
            pltpu.SemaphoreType.DMA((blocks,)),
            pltpu.SemaphoreType.DMA((len(w_parts),)),
        ],
        compiler_params=params(16),
        name="closing_pass",
    )(info, *toks, *w_parts, *sums, pinned(energy))


def grad_kernel(images, info_ref, rows_ref, own_ref, *refs):
    sums = refs[0:SIDE]
    (u, ut, w, e, keep_ref, *sends, loss_ref, soft_w, mass_w, acc, totals, soft_all,
     mass_all) = refs[SIDE:]
    blocks, slots, cols = e.shape
    totals[...] = added(rows_ref)
    own = own_ref[...]
    n = PER * blocks
    me = info_ref[0] * 2 + info_ref[1]
    mine = jnp.log(vector(totals, me, n)) - vector(totals, 0, 2 * n) / vector(totals, me)
    loss_ref[...] = jnp.where(vector(own_ref, me) > 0.0, mine, 0.0)
    weight = live_of(own) / (jnp.maximum(own, 1.0) * images) * (loss_scale / student_temp)
    soft_all[0:n, :] = weight[0:n] / totals[n : 2 * n, :]
    mass_all[0:n, :] = weight[0:n] / totals[0:n, :]
    c = column_factor(sums)
    inv = inverse_norms(w)
    scale = inv * (LOG2E / student_temp)
    acc[...] = jnp.zeros_like(acc)

    def step(s, _):
        for half in range(2):
            at = slice(half * slots, (half + 1) * slots)
            soft_w[at, :] = down(vector(soft_all, 2 * s + half))
            mass_w[at, :] = down(vector(mass_all, 2 * s + half))
        units = jnp.concatenate([ut[2 * s], ut[2 * s + 1]], axis=1)
        for n in chunks(cols, WIDE):
            raws = [nn(u[2 * s + half], w[:, n]) for half in range(2)]
            columns = []
            for i in range(0, WIDE, LANES):
                k = slice(n.start + i, n.start + i + LANES)
                parts = []
                for half in range(2):
                    b = 2 * s + half
                    for r in chunks(slots, ROWS):
                        at = slice(half * slots + r.start, half * slots + r.stop)
                        power = raws[half][r, i : i + LANES] * scale[:, k]
                        soft = jnp.exp2(power) * soft_w[at, :]
                        target = e[b, r, k].astype(f32) * c[:, k] * mass_w[at, :]
                        parts.append((soft - target).astype(bf16))
                columns.append(jnp.concatenate(parts, axis=0))
            acc[:, n] += nn(units, jnp.concatenate(columns, axis=1))
        return 0

    lax.fori_loop(0, blocks // 2, step, 0)
    grad = acc[...]
    unit = w[...].astype(f32) * inv
    dot = jnp.sum(grad * unit, axis=0, keepdims=True)
    acc[...] = inv * (grad - unit * dot)
    rows = keep_ref.shape[0]
    keep_ref[...] = acc[0:rows, :]
    for i, ref in enumerate(sends):
        ref[...] = acc[(i + 1) * rows : (i + 2) * rows, :].astype(bf16)


def grad_pass(images, info, rows, own, sums, u, ut, w, energy):
    blocks, slots, cols = energy.shape
    d = ut.shape[1]
    part = (d // SIDE, cols)
    return pl.pallas_call(
        functools.partial(grad_kernel, float(images)),
        out_shape=(shape(part), *[shape(part, bf16)] * len(SHIFTS), shape((PER, LANES))),
        in_specs=[SM] + [VM] * (SIDE + 6),
        out_specs=(VM,) * 5,
        scratch_shapes=[
            pltpu.VMEM((2 * slots, LANES), f32),
            pltpu.VMEM((2 * slots, LANES), f32),
            pltpu.VMEM((d, cols), f32),
            pltpu.VMEM(rows.shape[1:], f32),
            pltpu.VMEM((TALL, LANES), f32),
            pltpu.VMEM((TALL, LANES), f32),
        ],
        compiler_params=params(16),
        name="grad_pass",
    )(info, rows, own, *sums, u, ut, w, pinned(energy))


def shift(value, axis, k):
    n = lax.axis_size(axis)
    return lax.ppermute(value, axis, [(i, (i + k) % n) for i in range(n)])


def exchange(value, axes):
    return lax.all_to_all(value, axes, 0, 0, tiled=True)


def ring(value, axis):
    return [value] + [shift(value, axis, k) for k in SHIFTS]


def both_cores(blocks):
    return blocks + [shift(b, "c", 1) for b in blocks]


def local(teacher_feat, student_feat, teacher_proto, student_proto, mask_index, mask_count):
    slots = mask_index.shape[0]
    images = lax.axis_size(("z", "y", "c")) * (teacher_feat.shape[0] // PATCH)
    peers = lax.axis_size(GROUP)
    me = lax.axis_index(("z", "y", "c")).reshape(1)
    t_tok, s_tok, w, info = tokens(
        me, mask_count, mask_index, teacher_feat, student_feat, teacher_proto, student_proto
    )
    w = exchange(w, ("z", "c"))
    s_toks = ring(s_tok, "z")
    t_w, t_tok = split(0, w, t_tok, s_toks)
    t_parts = ring(t_w, "y")
    t_toks = both_cores(ring(t_tok, "z"))
    s_toks = both_cores(s_toks)
    s_w, _ = split(1, w, s_tok, t_parts)
    s_parts = ring(s_w, "y")
    energy, own, sums = energy_pass(info, t_toks, t_parts, slots, [s_w, *s_toks])
    for i in range(SWEEPS - 1):
        after = s_parts if i == 0 else []
        rows = exchange(row_pass(ring(sums, "y"), energy, peers, after), GROUP)
        sums = column_pass(rows, own, energy)
    sums = ring(sums, "y")
    s_u, s_ut, s_w, rows = closing_pass(info, s_toks, s_parts, sums, energy, peers)
    rows = exchange(rows, GROUP)
    keep, *sends, loss = grad_pass(images, info, rows, own, sums, s_u, s_ut, s_w, energy)
    for k, send in zip(SHIFTS, sends):
        keep = keep + shift(send, "y", -k).astype(f32)
    proto_grad = lax.all_to_all(keep, ("z", "c"), 0, 1, tiled=True)
    return (loss.reshape(-1), proto_grad)


def solution(mesh):
    parts = Mesh(mesh.devices.reshape(4, 4, 2, 4), ("z", "y", "c", "x"))
    dp = ("z", "y", "c")
    return jax.shard_map(
        local,
        mesh=parts,
        in_specs=(P(dp, None), P(dp, None), P(dp, "x"), P(dp, "x"), P(dp), P(dp)),
        out_specs=(P(dp), P(dp, "x")),
        check_vma=False,
    )
```

```python
import functools

import jax
import jax.numpy as jnp
from jax import lax
from jax.experimental import pallas as pl
from jax.experimental.pallas import tpu as pltpu
from jax.sharding import Mesh
from jax.sharding import PartitionSpec as P

PATCH = 256
SWEEPS = 3
EXTRA = 16
LOG2E = 1.4426950408889634
ROWS = 64
SURE = 192
WIDE = 256
PER = 3
TALL = 32
LANES = 128
SHIFTS = (1, 3, 2)
SIDE = 4
DP = ("z", "y", "c")
GROUP = ("z", "c", "x")

teacher_temp = 0.07
student_temp = 0.1
loss_scale = 65536.0

f32 = jnp.float32
bf16 = jnp.bfloat16

VM = pl.BlockSpec(memory_space=pltpu.VMEM)
SM = pl.BlockSpec(memory_space=pltpu.SMEM)
ANY = pl.BlockSpec(memory_space=pl.ANY)


def params(mib):
    return pltpu.CompilerParams(vmem_limit_bytes=mib * 1024 * 1024)


def pinned(array):
    return pltpu.with_memory_space_constraint(array, pltpu.VMEM)


def shape(dims, dtype=f32):
    return jax.ShapeDtypeStruct(dims, dtype)


def nn(a, b):
    return lax.dot_general(a, b, (((1,), (0,)), ((), ())), preferred_element_type=f32)


def tn(a, b):
    return lax.dot_general(a, b, (((0,), (0,)), ((), ())), preferred_element_type=f32)


def tokens_kernel(me_ref, count_ref, index_ref, teacher_ref, student_ref, tp_ref, sp_ref,
                  tok_out, w_out, info_out, feats, protos, sems, p_sems):
    proto_copies = [
        pltpu.make_async_copy(ref, protos.at[i], p_sems.at[i])
        for i, ref in enumerate((tp_ref, sp_ref))
    ]
    copies = [
        pltpu.make_async_copy(ref, feats.at[i], sems.at[i])
        for i, ref in enumerate((teacher_ref, student_ref))
    ]
    for c in proto_copies + copies:
        c.start()
    me = me_ref[0]
    y = (me >> 1) & 3
    info_out[0] = me >> 3
    info_out[1] = me & 1
    info_out[2] = y
    slots = index_ref.shape[0]
    source, d = feats.shape[1:]
    index_row = index_ref[...].reshape(1, slots)
    index_col = jnp.transpose(jnp.broadcast_to(index_row, (8, slots)))[:, 0:1]
    count = count_ref[0]
    live_row = lax.broadcasted_iota(jnp.int32, (1, slots), 1) < count
    live_col = lax.broadcasted_iota(jnp.int32, (slots, 1), 0) < count
    same = ((index_col >> 8) == (index_row >> 8)) & live_col
    own = jnp.sum(jnp.where(same, 1.0, 0.0), axis=0, keepdims=True)
    own = jnp.where(live_row, own, 0.0)
    rest = jnp.concatenate([own[:, d:], jnp.zeros((1, 2 * d - slots), f32)], axis=1)
    at = lax.broadcasted_iota(jnp.int32, (EXTRA, d), 0)
    counts = jnp.where(at == 0, own[:, 0:d], jnp.where(at == 1, rest, 0.0))
    tok_out[slots : slots + EXTRA, :] = counts.astype(bf16)
    pick = jnp.where(
        lax.broadcasted_iota(jnp.int32, (slots, source), 1) == index_col, 1.0, 0.0
    ).astype(bf16)
    to = lax.broadcasted_iota(jnp.int32, (1, d), 1)
    turn = to >> 6
    turn = jnp.where(turn == 2, 3, jnp.where(turn == 3, 2, turn))
    origin = (
        ((to >> 4) & 3) * 64 + ((y + 4 - turn) & 3) * 16 + ((to >> 3) & 1) * 8 + (to & 7)
    )
    order = jnp.where(
        lax.broadcasted_iota(jnp.int32, (d, d), 0) == origin, 1.0, 0.0
    ).astype(bf16)
    for c in proto_copies:
        c.wait()
    parts, _, width = w_out.shape
    for q in range(parts):
        lanes = slice(q * width, (q + 1) * width)
        w_out[q] = jnp.concatenate(
            [protos[0, :, lanes].astype(f32), protos[1, :, lanes].astype(f32)], axis=0
        ).astype(bf16)
    for i, at in enumerate((0, slots + EXTRA)):
        copies[i].wait()
        rows = nn(pick, feats[i])
        unit = rows * lax.rsqrt(jnp.sum(rows * rows, axis=1, keepdims=True) + 1e-06)
        tok_out[at : at + slots, :] = nn(unit.astype(bf16), order).astype(bf16)


def tokens(me, count, index, teacher_feat, student_feat, teacher_proto, student_proto):
    slots, (source, d) = index.shape[0], teacher_feat.shape
    rows, cols = teacher_proto.shape
    parts = 8
    return pl.pallas_call(
        tokens_kernel,
        out_shape=(
            shape((2 * slots + EXTRA, d), bf16),
            shape((parts, 2 * rows, cols // parts), bf16),
            shape((3,), jnp.int32),
        ),
        in_specs=[SM, SM, VM, ANY, ANY, ANY, ANY],
        out_specs=(VM, VM, SM),
        scratch_shapes=[
            pltpu.VMEM((2, source, d), bf16),
            pltpu.VMEM((2, rows, cols), bf16),
            pltpu.SemaphoreType.DMA((2,)),
            pltpu.SemaphoreType.DMA((2,)),
        ],
        compiler_params=params(56),
        name="token_rows",
    )(me, count, index, teacher_feat, student_feat, teacher_proto, student_proto)


def stack_kernel(info_ref, *refs):
    toks, (t_out, s_out) = refs[0:4], refs[-2:]
    rows = t_out.shape[1]
    for k, ref in zip((0,) + SHIFTS, toks):
        z = (info_ref[0] + 4 - k) & 3
        t_out[z] = ref[0:rows, :]
        s_out[z] = ref[rows:, :]


def stack(info, toks, slots, after):
    n, d = len(toks), toks[0].shape[1]
    return pl.pallas_call(
        stack_kernel,
        out_shape=(shape((n, slots + EXTRA, d), bf16), shape((n, slots, d), bf16)),
        in_specs=[SM] + [VM] * n + [ANY] * len(after),
        out_specs=(VM, VM),
        compiler_params=params(16),
        name="stack",
    )(info, *toks, *after)


def split_kernel(which, w_ref, *refs):
    out = refs[-1]
    parts, _, width = w_ref.shape
    rows = w_ref[...].astype(f32)[:, 8 * which : 8 * which + 8]
    out[...] = rows.reshape(parts * 8, width).astype(bf16)


def split(which, w, after=()):
    parts, rows, width = w.shape
    return pl.pallas_call(
        functools.partial(split_kernel, which),
        out_shape=shape((parts * rows // 2, width), bf16),
        in_specs=[VM] + [ANY] * len(after),
        out_specs=VM,
        compiler_params=params(16),
        name="split_rows",
    )(w, *after)


def token_copies(info_ref, refs, dst, sems):
    core = info_ref[1]
    return [
        pltpu.make_async_copy(
            ref.at[z], dst.at[2 * z + (1 - core if i else core)], sems.at[4 * i + z]
        )
        for i, ref in enumerate(refs)
        for z in range(4)
    ]


def weight_copies(refs, dst, sems):
    rows = refs[0].shape[0]
    return [
        pltpu.make_async_copy(ref, dst.at[pl.ds(i * rows, rows)], sems.at[i])
        for i, ref in enumerate(refs)
    ]


def inverse_norms(w_ref):
    wide = w_ref[...].astype(f32)
    return lax.rsqrt(jnp.sum(wide * wide, axis=0, keepdims=True) + 1e-06)


def down(rows):
    return jnp.concatenate(
        [
            jnp.transpose(jnp.broadcast_to(rows[j : j + 1, :], (LANES, LANES)))
            for j in range(rows.shape[0])
        ],
        axis=0,
    )


def across(parts_ref):
    return jnp.concatenate(
        [
            jnp.sum(jnp.transpose(parts_ref[j : j + LANES, :]), axis=0, keepdims=True)
            for j in range(0, parts_ref.shape[0], LANES)
        ],
        axis=0,
    )


def vector(ref, b, first=0):
    return ref[pl.ds(first + PER * b, PER), :]


def added(parts_ref):
    total = parts_ref[0].astype(f32)
    for i in range(1, parts_ref.shape[0]):
        total = total + parts_ref[i].astype(f32)
    return total


def live_of(own):
    return jnp.where(own > 0.0, 1.0, 0.0)


def column_factor(refs):
    total = refs[0][...]
    for ref in refs[1:]:
        total = total + ref[...]
    return 1.0 / total


def chunks(n, size):
    return [slice(at, at + size) for at in range(0, n, size)]


def energy_kernel(info_ref, *refs):
    toks, w_refs = refs[0:2], refs[2:6]
    e_ref, own_ref, sum_ref, u, w, live, acc, t_sems, w_sems = refs[-9:]
    blocks, slots, cols = e_ref.shape
    t_copies = token_copies(info_ref, toks, u, t_sems)
    w_copies = weight_copies(w_refs, w, w_sems)
    for c in t_copies + w_copies:
        c.start()
    for c in w_copies:
        c.wait()
    scale = inverse_norms(w) * (LOG2E / teacher_temp)
    acc[...] = jnp.zeros_like(acc)
    own_ref[...] = jnp.zeros_like(own_ref)
    for c in t_copies:
        c.wait()

    def step(b, _):
        counts = u[b, slots : slots + EXTRA, :].astype(f32)
        for j in range(PER):
            row, lane = divmod(j * LANES, counts.shape[1])
            own_ref[pl.ds(PER * b + j, 1), :] = counts[row : row + 1, lane : lane + LANES]
        live[...] = down(live_of(vector(own_ref, b)))
        for n in chunks(cols, WIDE):
            raw = nn(u[b, 0:slots, :], w[:, n])
            for i in range(0, WIDE, LANES):
                k = slice(n.start + i, n.start + i + LANES)
                total = acc[:, k]
                for r in chunks(slots, ROWS):
                    energy = jnp.exp2(raw[r, i : i + LANES] * scale[:, k])
                    e_ref[b, r, k] = energy.astype(bf16)
                    total = total + (energy * live[r, :] if r.stop > SURE else energy)
                acc[:, k] = total
        return 0

    lax.fori_loop(0, blocks, step, 0)
    sum_ref[...] = jnp.sum(acc[...], axis=0, keepdims=True)


def energy_pass(info, toks, w_parts, slots, after):
    d, cols = SIDE * w_parts[0].shape[0], w_parts[0].shape[1]
    blocks = 2 * toks[0].shape[0]
    return pl.pallas_call(
        energy_kernel,
        out_shape=(
            pltpu.VMEM((blocks, slots, cols), bf16),
            shape((TALL, LANES)),
            shape((1, cols)),
        ),
        in_specs=[SM] + [ANY] * (len(toks) + len(w_parts) + len(after)),
        out_specs=(VM, VM, VM),
        scratch_shapes=[
            pltpu.VMEM((blocks, slots + EXTRA, d), bf16),
            pltpu.VMEM((d, cols), bf16),
            pltpu.VMEM((slots, LANES), f32),
            pltpu.VMEM((ROWS, cols), f32),
            pltpu.SemaphoreType.DMA((blocks,)),
            pltpu.SemaphoreType.DMA((len(w_parts),)),
        ],
        compiler_params=params(16),
        cost_estimate=pl.CostEstimate(
            flops=2 * blocks * slots * cols * d,
            transcendentals=blocks * slots * cols,
            bytes_accessed=2 * blocks * slots * cols,
        ),
        name="energy_pass",
    )(info, *toks, *w_parts, *after)


def collect_kernel(info_ref, sums_ref, *refs):
    w_refs, toks, (sums_out, w_out, u_out) = refs[0:4], refs[4:6], refs[6:]
    sums_out[...] = sums_ref[...]
    rows = w_refs[0].shape[0]
    for i, ref in enumerate(w_refs):
        w_out[i * rows : (i + 1) * rows, :] = ref[...]
    core = info_ref[1]
    for i, ref in enumerate(toks):
        for z in range(ref.shape[0]):
            u_out[2 * z + (1 - core if i else core)] = ref[z]


def collect(info, sums, w_parts, toks):
    rows, cols = w_parts[0].shape
    n, slots, d = toks[0].shape
    return pl.pallas_call(
        collect_kernel,
        out_shape=(
            shape(sums.shape),
            shape((SIDE * rows, cols), bf16),
            shape((2 * n, slots, d), bf16),
        ),
        in_specs=[SM] + [VM] * (1 + len(w_parts) + len(toks)),
        out_specs=(VM, VM, VM),
        compiler_params=params(16),
        name="collect",
    )(info, sums, *w_parts, *toks)


def row_kernel(*refs):
    sums, e, (out_ref, part, rows) = refs[0:SIDE], refs[SIDE], refs[-3:]
    blocks, slots, cols = e.shape
    c = column_factor(sums)
    rows[...] = jnp.zeros_like(rows)

    def step(b, _):
        for r in chunks(slots, ROWS):
            total = jnp.zeros((ROWS, LANES), f32)
            for k in chunks(cols, LANES):
                total = total + e[b, r, k].astype(f32) * c[:, k]
            part[r, :] = total
        rows[pl.ds(PER * b, PER), :] = across(part)
        return 0

    lax.fori_loop(0, blocks, step, 0)
    low = rows[...].astype(bf16)
    for i in range(out_ref.shape[0]):
        out_ref[i] = low


def row_pass(sums, energy, peers, after=()):
    blocks, slots, cols = energy.shape
    return pl.pallas_call(
        row_kernel,
        out_shape=shape((peers, TALL, LANES), bf16),
        in_specs=[VM] * (SIDE + 1) + [ANY] * len(after),
        out_specs=VM,
        scratch_shapes=[pltpu.VMEM((slots, LANES), f32), pltpu.VMEM((TALL, LANES), f32)],
        compiler_params=params(8),
        name="row_pass",
    )(*sums, pinned(energy), *after)


def column_kernel(rows_ref, own_ref, e, out_ref, weight, ratio, acc):
    blocks, slots, cols = e.shape
    acc[...] = jnp.zeros_like(acc)
    own = own_ref[...]
    ratio[...] = live_of(own) / jnp.where(own > 0.0, added(rows_ref), 1.0)

    def step(b, _):
        weight[...] = down(vector(ratio, b))
        for k in chunks(cols, LANES):
            total = acc[:, k]
            for r in chunks(slots, ROWS):
                total = total + e[b, r, k].astype(f32) * weight[r, :]
            acc[:, k] = total
        return 0

    lax.fori_loop(0, blocks, step, 0)
    out_ref[...] = jnp.sum(acc[...], axis=0, keepdims=True)


def column_pass(rows, own, energy):
    blocks, slots, cols = energy.shape
    return pl.pallas_call(
        column_kernel,
        out_shape=shape((1, cols)),
        in_specs=[VM, VM, VM],
        out_specs=VM,
        scratch_shapes=[
            pltpu.VMEM((slots, LANES), f32),
            pltpu.VMEM((TALL, LANES), f32),
            pltpu.VMEM((ROWS, cols), f32),
        ],
        compiler_params=params(8),
        name="column_pass",
    )(rows, own, pinned(energy))


def softmax_kernel(first, u, w, out_ref, part):
    _, slots, _ = u.shape
    cols = w.shape[1]
    scale = inverse_norms(w) * (LOG2E / student_temp)

    def step(b, _):
        part[...] = jnp.zeros_like(part)
        for n in chunks(cols, cols // 2):
            raw = nn(u[first + b], w[:, n])
            for r in chunks(slots, ROWS):
                total = part[r, :]
                for i in range(0, cols // 2, LANES):
                    k = slice(n.start + i, n.start + i + LANES)
                    total = total + jnp.exp2(raw[r, i : i + LANES] * scale[:, k])
                part[r, :] = total
        out_ref[pl.ds(PER * b, PER), :] = across(part)
        return 0

    lax.fori_loop(0, out_ref.shape[0] // PER, step, 0)


def softmax_pass(u, w, first, count):
    blocks, slots, d = u.shape
    cols = w.shape[1]
    return pl.pallas_call(
        functools.partial(softmax_kernel, first),
        out_shape=shape((PER * count, LANES)),
        in_specs=[VM, VM],
        out_specs=VM,
        scratch_shapes=[pltpu.VMEM((slots, LANES), f32)],
        compiler_params=params(16),
        cost_estimate=pl.CostEstimate(
            flops=2 * count * slots * cols * d,
            transcendentals=count * slots * cols,
            bytes_accessed=count * slots * d,
        ),
        name="softmax_pass",
    )(u, w)


def closing_kernel(*refs):
    u, w, soft_a, soft_b, sums = refs[0], refs[1], refs[2], refs[3], refs[4 : 4 + SIDE]
    e, ut, out_ref, part, rows, crosses = refs[4 + SIDE :]
    blocks, slots, cols = e.shape
    c = column_factor(sums)
    cs = c * (inverse_norms(w) * (1.0 / student_temp))
    rows[...] = jnp.zeros_like(rows)
    half = PER * blocks // 2
    rows[2 * half : 3 * half, :] = soft_a[...]
    rows[3 * half : 4 * half, :] = soft_b[...]

    def step(b, _):
        ut[b] = jnp.transpose(u[b].astype(f32)).astype(bf16)
        part[...] = jnp.zeros_like(part)
        for n in chunks(cols, cols // 2):
            raw = nn(u[b], w[:, n])
            for r in chunks(slots, ROWS):
                mass, cross = part[0, r, :], part[1, r, :]
                for i in range(0, cols // 2, LANES):
                    k = slice(n.start + i, n.start + i + LANES)
                    energy = e[b, r, k].astype(f32)
                    mass = mass + energy * c[:, k]
                    cross = cross + energy * cs[:, k] * raw[r, i : i + LANES]
                part[0, r, :], part[1, r, :] = mass, cross
        rows[pl.ds(PER * b, PER), :] = across(part.at[0])
        crosses[b, 0:PER, :] = across(part.at[1])
        return 0

    lax.fori_loop(0, blocks, step, 0)
    at = 2 * PER * blocks
    for i in range(out_ref.shape[0]):
        rows[at : at + PER, :] = crosses[i // 4, 0:PER, :]
        out_ref[i] = rows[...].astype(bf16)


def closing_pass(u, w, soft, sums, energy, peers):
    blocks, slots, cols = energy.shape
    d = w.shape[0]
    return pl.pallas_call(
        closing_kernel,
        out_shape=(
            pltpu.VMEM((blocks, d, slots), bf16),
            shape((peers, 2 * TALL, LANES), bf16),
        ),
        in_specs=[VM] * (SIDE + 5),
        out_specs=(VM, VM),
        scratch_shapes=[
            pltpu.VMEM((2, slots, LANES), f32),
            pltpu.VMEM((2 * TALL, LANES), f32),
            pltpu.VMEM((blocks, 8, LANES), f32),
        ],
        compiler_params=params(16),
        name="closing_pass",
    )(u, w, *soft, *sums, pinned(energy))


def grad_kernel(images, info_ref, rows_ref, own_ref, *refs):
    sums = refs[0:SIDE]
    (u, ut, w, e, out_ref, loss_ref, soft_w, mass_w, acc, totals, soft_all,
     mass_all) = refs[SIDE:]
    blocks, slots, cols = e.shape
    totals[...] = added(rows_ref)
    own = own_ref[...]
    n = PER * blocks
    me = info_ref[0] * 2 + info_ref[1]
    mine = jnp.log(vector(totals, me, n)) - vector(totals, 0, 2 * n) / vector(totals, me)
    loss_ref[...] = jnp.where(vector(own_ref, me) > 0.0, mine, 0.0)
    weight = live_of(own) / (jnp.maximum(own, 1.0) * images) * (loss_scale / student_temp)
    soft_all[0:n, :] = weight[0:n] / totals[n : 2 * n, :]
    mass_all[0:n, :] = weight[0:n] / totals[0:n, :]
    c = column_factor(sums)
    inv = inverse_norms(w)
    scale = inv * (LOG2E / student_temp)
    acc[...] = jnp.zeros_like(acc)

    def step(s, _):
        for half in range(2):
            at = slice(half * slots, (half + 1) * slots)
            soft_w[at, :] = down(vector(soft_all, 2 * s + half))
            mass_w[at, :] = down(vector(mass_all, 2 * s + half))
        units = jnp.concatenate([ut[2 * s], ut[2 * s + 1]], axis=1)
        for n in chunks(cols, WIDE):
            raws = [nn(u[2 * s + half], w[:, n]) for half in range(2)]
            parts = []
            for half in range(2):
                b = 2 * s + half
                for r in chunks(slots, ROWS):
                    at = slice(half * slots + r.start, half * slots + r.stop)
                    soft_r, mass_r = soft_w[at, :], mass_w[at, :]
                    line = []
                    for i in range(0, WIDE, LANES):
                        k = slice(n.start + i, n.start + i + LANES)
                        power = raws[half][r, i : i + LANES] * scale[:, k]
                        target = e[b, r, k].astype(f32) * c[:, k] * mass_r
                        line.append((jnp.exp2(power) * soft_r - target).astype(bf16))
                    parts.append(jnp.concatenate(line, axis=1))
            acc[:, n] += nn(units, jnp.concatenate(parts, axis=0))
        return 0

    lax.fori_loop(0, blocks // 2, step, 0)
    grad = acc[...]
    unit = w[...].astype(f32) * inv
    dot = jnp.sum(grad * unit, axis=0, keepdims=True)
    acc[...] = inv * (grad - unit * dot)
    rows = out_ref.shape[1]
    for i, k in enumerate((0,) + SHIFTS):
        y = (info_ref[2] + 4 - k) & 3
        for q in range(8):
            at = (8 * i + q) * rows
            out_ref[(q // 2) * 8 + 2 * y + q % 2] = acc[at : at + rows, :].astype(bf16)


def grad_pass(images, info, rows, own, sums, u, ut, w, energy, peers):
    blocks, slots, cols = energy.shape
    d = ut.shape[1]
    return pl.pallas_call(
        functools.partial(grad_kernel, float(images)),
        out_shape=(shape((peers, d // peers, cols), bf16), shape((PER, LANES))),
        in_specs=[SM] + [VM] * (SIDE + 6),
        out_specs=(VM, VM),
        scratch_shapes=[
            pltpu.VMEM((2 * slots, LANES), f32),
            pltpu.VMEM((2 * slots, LANES), f32),
            pltpu.VMEM((d, cols), f32),
            pltpu.VMEM(rows.shape[1:], f32),
            pltpu.VMEM((TALL, LANES), f32),
            pltpu.VMEM((TALL, LANES), f32),
        ],
        compiler_params=params(16),
        name="grad_pass",
    )(info, rows, own, *sums, u, ut, w, pinned(energy))


def sum_kernel(parts_ref, out_ref):
    peers, _, width = parts_ref.shape
    for q in range(peers // SIDE):
        first = (q // 2) * 2 * SIDE + q % 2
        total = parts_ref[first].astype(f32)
        for y in range(1, SIDE):
            total = total + parts_ref[first + 2 * y].astype(f32)
        out_ref[:, q * width : (q + 1) * width] = total


def sum_pass(parts):
    peers, rows, width = parts.shape
    return pl.pallas_call(
        sum_kernel,
        out_shape=shape((rows, peers // SIDE * width)),
        in_specs=[VM],
        out_specs=VM,
        compiler_params=params(16),
        name="sum_pass",
    )(parts)


def shift(value, axis, k):
    n = lax.axis_size(axis)
    return lax.ppermute(value, axis, [(i, (i + k) % n) for i in range(n)])


def exchange(value, axes):
    return lax.all_to_all(value, axes, 0, 0, tiled=True)


def ring(value, axis):
    return [value] + [shift(value, axis, k) for k in SHIFTS]


def local(teacher_feat, student_feat, teacher_proto, student_proto, mask_index, mask_count):
    slots = mask_index.shape[0]
    images = lax.axis_size(DP) * (teacher_feat.shape[0] // PATCH)
    peers = lax.axis_size(GROUP)
    me = lax.axis_index(DP).reshape(1)
    tok, w, info = tokens(
        me, mask_count, mask_index, teacher_feat, student_feat, teacher_proto, student_proto
    )
    w = exchange(w, ("z", "c"))
    t_parts = ring(split(0, w), "y")
    t_mine, s_mine = stack(info, ring(tok, "z"), slots, t_parts[1:])
    t_toks, s_toks = ([v, shift(v, "c", 1)] for v in (t_mine, s_mine))
    s_parts = ring(split(1, w, t_parts[1:]), "y")
    energy, own, sums = energy_pass(info, t_toks, t_parts, slots, s_parts[:1])
    sums, s_w, s_u = collect(info, sums, s_parts, s_toks)
    half = s_u.shape[0] // 2
    soft = []
    for _ in range(SWEEPS - 1):
        rows = row_pass(ring(sums, "y"), energy, peers, soft)
        soft.append(softmax_pass(s_u, s_w, half * len(soft), half))
        sums = column_pass(exchange(rows, GROUP), own, energy)
    ring_sums = ring(sums, "y")
    s_ut, rows = closing_pass(s_u, s_w, soft, ring_sums, energy, peers)
    rows = exchange(rows, GROUP)
    grad, loss = grad_pass(
        images, info, rows, own, ring_sums, s_u, s_ut, s_w, energy, lax.axis_size(DP)
    )
    return (loss.reshape(-1), sum_pass(exchange(grad, DP)))


def solution(mesh):
    parts = Mesh(mesh.devices.reshape(4, 4, 2, 4), ("z", "y", "c", "x"))
    return jax.shard_map(
        local,
        mesh=parts,
        in_specs=(P(DP, None), P(DP, None), P(DP, "x"), P(DP, "x"), P(DP), P(DP)),
        out_specs=(P(DP), P(DP, "x")),
        check_vma=False,
    )
```

```python
import functools

import jax
import jax.numpy as jnp
from jax import lax
from jax.experimental import pallas as pl
from jax.experimental.pallas import tpu as pltpu
from jax.sharding import Mesh
from jax.sharding import PartitionSpec as P

PATCH = 256
SWEEPS = 3
EXTRA = 16
LOG2E = 1.4426950408889634
ROWS = 64
SURE = 192
WIDE = 256
PER = 3
HALF = 16
TALL = 32
LANES = 128
SHIFTS = (1, 3, 2)
SIDE = 4
DP = ("z", "y", "c")
GROUP = ("z", "c", "x")

teacher_temp = 0.07
student_temp = 0.1
loss_scale = 65536.0

f32 = jnp.float32
bf16 = jnp.bfloat16

VM = pl.BlockSpec(memory_space=pltpu.VMEM)
SM = pl.BlockSpec(memory_space=pltpu.SMEM)
ANY = pl.BlockSpec(memory_space=pl.ANY)


def params(mib):
    return pltpu.CompilerParams(vmem_limit_bytes=mib * 1024 * 1024)


def pinned(array):
    return pltpu.with_memory_space_constraint(array, pltpu.VMEM)


def shape(dims, dtype=f32):
    return jax.ShapeDtypeStruct(dims, dtype)


def nn(a, b):
    return lax.dot_general(a, b, (((1,), (0,)), ((), ())), preferred_element_type=f32)


def tn(a, b):
    return lax.dot_general(a, b, (((0,), (0,)), ((), ())), preferred_element_type=f32)


def tokens_kernel(me_ref, count_ref, index_ref, teacher_ref, student_ref, tp_ref, sp_ref,
                  tok_out, w_out, info_out, feats, protos, sems, p_sems):
    proto_copies = [
        pltpu.make_async_copy(ref, protos.at[i], p_sems.at[i])
        for i, ref in enumerate((tp_ref, sp_ref))
    ]
    copies = [
        pltpu.make_async_copy(ref, feats.at[i], sems.at[i])
        for i, ref in enumerate((teacher_ref, student_ref))
    ]
    for c in proto_copies + copies:
        c.start()
    me = me_ref[0]
    y = (me >> 1) & 3
    info_out[0] = me >> 3
    info_out[1] = me & 1
    info_out[2] = y
    slots = index_ref.shape[0]
    source, d = feats.shape[1:]
    index_row = index_ref[...].reshape(1, slots)
    index_col = jnp.transpose(jnp.broadcast_to(index_row, (8, slots)))[:, 0:1]
    count = count_ref[0]
    live_row = lax.broadcasted_iota(jnp.int32, (1, slots), 1) < count
    live_col = lax.broadcasted_iota(jnp.int32, (slots, 1), 0) < count
    same = ((index_col >> 8) == (index_row >> 8)) & live_col
    own = jnp.sum(jnp.where(same, 1.0, 0.0), axis=0, keepdims=True)
    own = jnp.where(live_row, own, 0.0)
    rest = jnp.concatenate([own[:, d:], jnp.zeros((1, 2 * d - slots), f32)], axis=1)
    at = lax.broadcasted_iota(jnp.int32, (EXTRA, d), 0)
    counts = jnp.where(at == 0, own[:, 0:d], jnp.where(at == 1, rest, 0.0))
    tok_out[slots : slots + EXTRA, :] = counts.astype(bf16)
    pick = jnp.where(
        lax.broadcasted_iota(jnp.int32, (slots, source), 1) == index_col, 1.0, 0.0
    ).astype(bf16)
    to = lax.broadcasted_iota(jnp.int32, (1, d), 1)
    turn = to >> 6
    turn = jnp.where(turn == 2, 3, jnp.where(turn == 3, 2, turn))
    origin = (
        ((to >> 4) & 3) * 64 + ((y + 4 - turn) & 3) * 16 + ((to >> 3) & 1) * 8 + (to & 7)
    )
    order = jnp.where(
        lax.broadcasted_iota(jnp.int32, (d, d), 0) == origin, 1.0, 0.0
    ).astype(bf16)
    for c in proto_copies:
        c.wait()
    parts, _, width = w_out.shape
    for q in range(parts):
        lanes = slice(q * width, (q + 1) * width)
        w_out[q] = jnp.concatenate(
            [protos[0, :, lanes].astype(f32), protos[1, :, lanes].astype(f32)], axis=0
        ).astype(bf16)
    for i, at in enumerate((0, slots + EXTRA)):
        copies[i].wait()
        rows = nn(pick, feats[i])
        unit = rows * lax.rsqrt(jnp.sum(rows * rows, axis=1, keepdims=True) + 1e-06)
        tok_out[at : at + slots, :] = nn(unit.astype(bf16), order).astype(bf16)


def tokens(me, count, index, teacher_feat, student_feat, teacher_proto, student_proto):
    slots, (source, d) = index.shape[0], teacher_feat.shape
    rows, cols = teacher_proto.shape
    parts = 8
    return pl.pallas_call(
        tokens_kernel,
        out_shape=(
            shape((2 * slots + EXTRA, d), bf16),
            shape((parts, 2 * rows, cols // parts), bf16),
            shape((3,), jnp.int32),
        ),
        in_specs=[SM, SM, VM, ANY, ANY, ANY, ANY],
        out_specs=(VM, VM, SM),
        scratch_shapes=[
            pltpu.VMEM((2, source, d), bf16),
            pltpu.VMEM((2, rows, cols), bf16),
            pltpu.SemaphoreType.DMA((2,)),
            pltpu.SemaphoreType.DMA((2,)),
        ],
        compiler_params=params(56),
        name="token_rows",
    )(me, count, index, teacher_feat, student_feat, teacher_proto, student_proto)


def stack_kernel(info_ref, *refs):
    toks, (t_out, s_out) = refs[0:4], refs[-2:]
    rows = t_out.shape[1]
    for k, ref in zip((0,) + SHIFTS, toks):
        z = (info_ref[0] + 4 - k) & 3
        t_out[z] = ref[0:rows, :]
        s_out[z] = ref[rows:, :]


def stack(info, toks, slots, after):
    n, d = len(toks), toks[0].shape[1]
    return pl.pallas_call(
        stack_kernel,
        out_shape=(shape((n, slots + EXTRA, d), bf16), shape((n, slots, d), bf16)),
        in_specs=[SM] + [VM] * n + [ANY] * len(after),
        out_specs=(VM, VM),
        compiler_params=params(16),
        name="stack",
    )(info, *toks, *after)


def split_kernel(which, w_ref, *refs):
    out = refs[-1]
    parts, _, width = w_ref.shape
    rows = w_ref[...].astype(f32)[:, 8 * which : 8 * which + 8]
    out[...] = rows.reshape(parts * 8, width).astype(bf16)


def split(which, w, after=()):
    parts, rows, width = w.shape
    return pl.pallas_call(
        functools.partial(split_kernel, which),
        out_shape=shape((parts * rows // 2, width), bf16),
        in_specs=[VM] + [ANY] * len(after),
        out_specs=VM,
        compiler_params=params(16),
        name="split_rows",
    )(w, *after)


def place(info_ref, refs, dst):
    core = info_ref[1]
    for i, ref in enumerate(refs):
        for z in range(ref.shape[0]):
            dst[2 * z + (1 - core if i else core)] = ref[z]


def lay(refs, dst):
    rows = refs[0].shape[0]
    for i, ref in enumerate(refs):
        dst[i * rows : (i + 1) * rows, :] = ref[...]


def inverse_norms(w_ref):
    wide = w_ref[...].astype(f32)
    return lax.rsqrt(jnp.sum(wide * wide, axis=0, keepdims=True) + 1e-06)


def down(rows):
    return jnp.concatenate(
        [
            jnp.transpose(jnp.broadcast_to(rows[j : j + 1, :], (LANES, LANES)))
            for j in range(rows.shape[0])
        ],
        axis=0,
    )


def across(parts_ref):
    return jnp.concatenate(
        [
            jnp.sum(jnp.transpose(parts_ref[j : j + LANES, :]), axis=0, keepdims=True)
            for j in range(0, parts_ref.shape[0], LANES)
        ],
        axis=0,
    )


def vector(ref, b, first=0):
    return ref[pl.ds(first + PER * b, PER), :]


def added(parts_ref):
    total = parts_ref[0].astype(f32)
    for i in range(1, parts_ref.shape[0]):
        total = total + parts_ref[i].astype(f32)
    return total


def live_of(own):
    return jnp.where(own > 0.0, 1.0, 0.0)


def column_factor(refs):
    total = refs[0][...]
    for ref in refs[1:]:
        total = total + ref[...]
    return 1.0 / total


def chunks(n, size):
    return [slice(at, at + size) for at in range(0, n, size)]


def energy_kernel(info_ref, *refs):
    toks, w_refs = refs[0:2], refs[2:6]
    e_ref, own_ref, sum_ref, u, w, live, acc = refs[-7:]
    blocks, slots, cols = e_ref.shape
    place(info_ref, toks, u)
    lay(w_refs, w)
    scale = inverse_norms(w) * (LOG2E / teacher_temp)
    acc[...] = jnp.zeros_like(acc)
    own_ref[...] = jnp.zeros_like(own_ref)

    def step(b, _):
        counts = u[b, slots : slots + EXTRA, :].astype(f32)
        for j in range(PER):
            row, lane = divmod(j * LANES, counts.shape[1])
            own_ref[pl.ds(PER * b + j, 1), :] = counts[row : row + 1, lane : lane + LANES]
        live[...] = down(live_of(vector(own_ref, b)))
        for n in chunks(cols, WIDE):
            raw = nn(u[b, 0:slots, :], w[:, n])
            for i in range(0, WIDE, LANES):
                k = slice(n.start + i, n.start + i + LANES)
                total = acc[:, k]
                for r in chunks(slots, ROWS):
                    energy = jnp.exp2(raw[r, i : i + LANES] * scale[:, k])
                    e_ref[b, r, k] = energy.astype(bf16)
                    total = total + (energy * live[r, :] if r.stop > SURE else energy)
                acc[:, k] = total
        return 0

    lax.fori_loop(0, blocks, step, 0)
    sum_ref[...] = jnp.sum(acc[...], axis=0, keepdims=True)


def energy_pass(info, toks, w_parts, slots, after):
    d, cols = SIDE * w_parts[0].shape[0], w_parts[0].shape[1]
    blocks = 2 * toks[0].shape[0]
    return pl.pallas_call(
        energy_kernel,
        out_shape=(
            pltpu.VMEM((blocks, slots, cols), bf16),
            shape((TALL, LANES)),
            shape((1, cols)),
        ),
        in_specs=[SM] + [VM] * (len(toks) + len(w_parts)) + [ANY] * len(after),
        out_specs=(VM, VM, VM),
        scratch_shapes=[
            pltpu.VMEM((blocks, slots + EXTRA, d), bf16),
            pltpu.VMEM((d, cols), bf16),
            pltpu.VMEM((slots, LANES), f32),
            pltpu.VMEM((ROWS, cols), f32),
        ],
        compiler_params=params(16),
        cost_estimate=pl.CostEstimate(
            flops=2 * blocks * slots * cols * d,
            transcendentals=blocks * slots * cols,
            bytes_accessed=2 * blocks * slots * cols,
        ),
        name="energy_pass",
    )(info, *toks, *w_parts, *after)


def collect_kernel(info_ref, sums_ref, *refs):
    w_refs, toks, (sums_out, w_out, u_out) = refs[0:4], refs[4:6], refs[6:]
    sums_out[...] = sums_ref[...]
    lay(w_refs, w_out)
    place(info_ref, toks, u_out)


def collect(info, sums, w_parts, toks):
    rows, cols = w_parts[0].shape
    n, slots, d = toks[0].shape
    return pl.pallas_call(
        collect_kernel,
        out_shape=(
            shape(sums.shape),
            shape((SIDE * rows, cols), bf16),
            shape((2 * n, slots, d), bf16),
        ),
        in_specs=[SM] + [VM] * (1 + len(w_parts) + len(toks)),
        out_specs=(VM, VM, VM),
        compiler_params=params(16),
        name="collect",
    )(info, sums, *w_parts, *toks)


def row_kernel(*refs):
    sums, e, extra = refs[0:SIDE], refs[SIDE], refs[SIDE + 1 : -3]
    out_ref, part, rows = refs[-3:]
    blocks, slots, cols = e.shape
    c = column_factor(sums)
    rows[...] = jnp.zeros_like(rows)

    def step(b, _):
        for r in chunks(slots, ROWS):
            total = jnp.zeros((ROWS, LANES), f32)
            for k in chunks(cols, LANES):
                total = total + e[b, r, k].astype(f32) * c[:, k]
            part[r, :] = total
        rows[pl.ds(PER * b, PER), :] = across(part)
        return 0

    lax.fori_loop(0, blocks, step, 0)
    at = PER * blocks
    for ref in extra:
        end = at + ref.shape[0]
        if end <= rows.shape[0]:
            rows[at:end, :] = ref[...]
        at = end
    low = rows[...].astype(bf16)
    for i in range(out_ref.shape[0]):
        out_ref[i] = low


def row_pass(sums, energy, peers, tall, extra):
    blocks, slots, cols = energy.shape
    return pl.pallas_call(
        row_kernel,
        out_shape=shape((peers, tall, LANES), bf16),
        in_specs=[VM] * (SIDE + 1 + len(extra)),
        out_specs=VM,
        scratch_shapes=[pltpu.VMEM((slots, LANES), f32), pltpu.VMEM((tall, LANES), f32)],
        compiler_params=params(8),
        name="row_pass",
    )(*sums, pinned(energy), *extra)


def column_kernel(rows_ref, own_ref, e, out_ref, weight, ratio, acc):
    blocks, slots, cols = e.shape
    acc[...] = jnp.zeros_like(acc)
    own = own_ref[...]
    total = added(rows_ref)[0 : own.shape[0]]
    ratio[...] = live_of(own) / jnp.where(own > 0.0, total, 1.0)

    def step(b, _):
        weight[...] = down(vector(ratio, b))
        for k in chunks(cols, LANES):
            total = acc[:, k]
            for r in chunks(slots, ROWS):
                total = total + e[b, r, k].astype(f32) * weight[r, :]
            acc[:, k] = total
        return 0

    lax.fori_loop(0, blocks, step, 0)
    out_ref[...] = jnp.sum(acc[...], axis=0, keepdims=True)


def column_pass(rows, own, energy):
    blocks, slots, cols = energy.shape
    return pl.pallas_call(
        column_kernel,
        out_shape=shape((1, cols)),
        in_specs=[VM, VM, VM],
        out_specs=VM,
        scratch_shapes=[
            pltpu.VMEM((slots, LANES), f32),
            pltpu.VMEM((TALL, LANES), f32),
            pltpu.VMEM((ROWS, cols), f32),
        ],
        compiler_params=params(8),
        name="column_pass",
    )(rows, own, pinned(energy))


def softmax_kernel(first, u, w, out_ref, part):
    _, slots, _ = u.shape
    cols = w.shape[1]
    scale = inverse_norms(w) * (LOG2E / student_temp)

    def step(b, _):
        part[...] = jnp.zeros_like(part)
        for n in chunks(cols, cols // 2):
            raw = nn(u[first + b], w[:, n])
            for r in chunks(slots, ROWS):
                total = part[r, :]
                for i in range(0, cols // 2, LANES):
                    k = slice(n.start + i, n.start + i + LANES)
                    total = total + jnp.exp2(raw[r, i : i + LANES] * scale[:, k])
                part[r, :] = total
        out_ref[pl.ds(PER * b, PER), :] = across(part)
        return 0

    lax.fori_loop(0, out_ref.shape[0] // PER, step, 0)


def softmax_pass(u, w, first, count):
    blocks, slots, d = u.shape
    cols = w.shape[1]
    return pl.pallas_call(
        functools.partial(softmax_kernel, first),
        out_shape=shape((PER * count, LANES)),
        in_specs=[VM, VM],
        out_specs=VM,
        scratch_shapes=[pltpu.VMEM((slots, LANES), f32)],
        compiler_params=params(16),
        cost_estimate=pl.CostEstimate(
            flops=2 * count * slots * cols * d,
            transcendentals=count * slots * cols,
            bytes_accessed=count * slots * d,
        ),
        name="softmax_pass",
    )(u, w)


def closing_kernel(u, w, *refs):
    sums, (e, ut, out_ref, part, rows, crosses) = refs[0:SIDE], refs[SIDE:]
    blocks, slots, cols = e.shape
    c = column_factor(sums)
    cs = c * (inverse_norms(w) * (1.0 / student_temp))
    rows[...] = jnp.zeros_like(rows)

    def step(b, _):
        ut[b] = jnp.transpose(u[b].astype(f32)).astype(bf16)
        part[...] = jnp.zeros_like(part)
        for n in chunks(cols, cols // 2):
            raw = nn(u[b], w[:, n])
            for r in chunks(slots, ROWS):
                mass, cross = part[0, r, :], part[1, r, :]
                for i in range(0, cols // 2, LANES):
                    k = slice(n.start + i, n.start + i + LANES)
                    energy = e[b, r, k].astype(f32)
                    mass = mass + energy * c[:, k]
                    cross = cross + energy * cs[:, k] * raw[r, i : i + LANES]
                part[0, r, :], part[1, r, :] = mass, cross
        rows[pl.ds(PER * b, PER), :] = across(part.at[0])
        crosses[b, 0:PER, :] = across(part.at[1])
        return 0

    lax.fori_loop(0, blocks, step, 0)
    at = PER * blocks
    for i in range(out_ref.shape[0]):
        rows[at : at + PER, :] = crosses[i // 4, 0:PER, :]
        out_ref[i] = rows[...].astype(bf16)


def closing_pass(u, w, sums, energy, peers):
    blocks, slots, cols = energy.shape
    d = w.shape[0]
    return pl.pallas_call(
        closing_kernel,
        out_shape=(
            pltpu.VMEM((blocks, d, slots), bf16),
            shape((peers, TALL, LANES), bf16),
        ),
        in_specs=[VM] * (SIDE + 3),
        out_specs=(VM, VM),
        scratch_shapes=[
            pltpu.VMEM((2, slots, LANES), f32),
            pltpu.VMEM((TALL, LANES), f32),
            pltpu.VMEM((blocks, 8, LANES), f32),
        ],
        compiler_params=params(16),
        name="closing_pass",
    )(u, w, *sums, pinned(energy))


def grad_kernel(images, info_ref, rows_ref, softs_ref, own_ref, *refs):
    sums = refs[0:SIDE]
    (u, ut, w, e, out_ref, loss_ref, soft_w, mass_w, acc, totals, soft_all,
     mass_all) = refs[SIDE:]
    blocks, slots, cols = e.shape
    totals[...] = added(rows_ref)
    own = own_ref[...]
    n = PER * blocks
    me = info_ref[0] * 2 + info_ref[1]
    soft_all[0:n, :] = added(softs_ref)[n : 2 * n]
    mine = jnp.log(vector(soft_all, me)) - vector(totals, 0, n) / vector(totals, me)
    loss_ref[...] = jnp.where(vector(own_ref, me) > 0.0, mine, 0.0)
    weight = live_of(own) / (jnp.maximum(own, 1.0) * images) * (loss_scale / student_temp)
    soft_all[0:n, :] = weight[0:n] / soft_all[0:n, :]
    mass_all[0:n, :] = weight[0:n] / totals[0:n, :]
    c = column_factor(sums)
    inv = inverse_norms(w)
    scale = inv * (LOG2E / student_temp)
    acc[...] = jnp.zeros_like(acc)

    def step(s, _):
        for half in range(2):
            at = slice(half * slots, (half + 1) * slots)
            soft_w[at, :] = down(vector(soft_all, 2 * s + half))
            mass_w[at, :] = down(vector(mass_all, 2 * s + half))
        units = jnp.concatenate([ut[2 * s], ut[2 * s + 1]], axis=1)
        for n in chunks(cols, WIDE):
            raws = [nn(u[2 * s + half], w[:, n]) for half in range(2)]
            parts = []
            for half in range(2):
                b = 2 * s + half
                for r in chunks(slots, ROWS):
                    at = slice(half * slots + r.start, half * slots + r.stop)
                    soft_r, mass_r = soft_w[at, :], mass_w[at, :]
                    line = []
                    for i in range(0, WIDE, LANES):
                        k = slice(n.start + i, n.start + i + LANES)
                        power = raws[half][r, i : i + LANES] * scale[:, k]
                        target = e[b, r, k].astype(f32) * c[:, k] * mass_r
                        line.append((jnp.exp2(power) * soft_r - target).astype(bf16))
                    parts.append(jnp.concatenate(line, axis=1))
            acc[:, n] += nn(units, jnp.concatenate(parts, axis=0))
        return 0

    lax.fori_loop(0, blocks // 2, step, 0)
    grad = acc[...]
    unit = w[...].astype(f32) * inv
    dot = jnp.sum(grad * unit, axis=0, keepdims=True)
    acc[...] = inv * (grad - unit * dot)
    rows = out_ref.shape[1]
    for i, k in enumerate((0,) + SHIFTS):
        y = (info_ref[2] + 4 - k) & 3
        for q in range(8):
            at = (8 * i + q) * rows
            out_ref[(q // 2) * 8 + 2 * y + q % 2] = acc[at : at + rows, :].astype(bf16)


def grad_pass(images, info, rows, softs, own, sums, u, ut, w, energy, peers):
    blocks, slots, cols = energy.shape
    d = ut.shape[1]
    return pl.pallas_call(
        functools.partial(grad_kernel, float(images)),
        out_shape=(shape((peers, d // peers, cols), bf16), shape((PER, LANES))),
        in_specs=[SM] + [VM] * (SIDE + 7),
        out_specs=(VM, VM),
        scratch_shapes=[
            pltpu.VMEM((2 * slots, LANES), f32),
            pltpu.VMEM((2 * slots, LANES), f32),
            pltpu.VMEM((d, cols), f32),
            pltpu.VMEM((TALL, LANES), f32),
            pltpu.VMEM((TALL, LANES), f32),
            pltpu.VMEM((TALL, LANES), f32),
        ],
        compiler_params=params(16),
        name="grad_pass",
    )(info, rows, softs, own, *sums, u, ut, w, pinned(energy))


def sum_kernel(parts_ref, out_ref):
    peers, _, width = parts_ref.shape
    for q in range(peers // SIDE):
        first = (q // 2) * 2 * SIDE + q % 2
        total = parts_ref[first].astype(f32)
        for y in range(1, SIDE):
            total = total + parts_ref[first + 2 * y].astype(f32)
        out_ref[:, q * width : (q + 1) * width] = total


def sum_pass(parts):
    peers, rows, width = parts.shape
    return pl.pallas_call(
        sum_kernel,
        out_shape=shape((rows, peers // SIDE * width)),
        in_specs=[VM],
        out_specs=VM,
        compiler_params=params(16),
        name="sum_pass",
    )(parts)


def shift(value, axis, k):
    n = lax.axis_size(axis)
    return lax.ppermute(value, axis, [(i, (i + k) % n) for i in range(n)])


def exchange(value, axes):
    return lax.all_to_all(value, axes, 0, 0, tiled=True)


def ring(value, axis):
    return [value] + [shift(value, axis, k) for k in SHIFTS]


def local(teacher_feat, student_feat, teacher_proto, student_proto, mask_index, mask_count):
    slots = mask_index.shape[0]
    images = lax.axis_size(DP) * (teacher_feat.shape[0] // PATCH)
    peers = lax.axis_size(GROUP)
    me = lax.axis_index(DP).reshape(1)
    tok, w, info = tokens(
        me, mask_count, mask_index, teacher_feat, student_feat, teacher_proto, student_proto
    )
    w = exchange(w, ("z", "c"))
    t_parts = ring(split(0, w), "y")
    t_mine, s_mine = stack(info, ring(tok, "z"), slots, t_parts[1:])
    t_toks, s_toks = ([v, shift(v, "c", 1)] for v in (t_mine, s_mine))
    s_parts = ring(split(1, w, t_parts[1:]), "y")
    energy, own, sums = energy_pass(info, t_toks, t_parts, slots, s_parts[:1])
    sums, s_w, s_u = collect(info, sums, s_parts, s_toks)
    half = s_u.shape[0] // 2
    soft = []
    for i in range(SWEEPS - 1):
        soft.append(softmax_pass(s_u, s_w, half * i, half))
        tall = TALL if i < SWEEPS - 2 else TALL + HALF
        rows = exchange(row_pass(ring(sums, "y"), energy, peers, tall, soft), GROUP)
        sums = column_pass(rows, own, energy)
    ring_sums = ring(sums, "y")
    s_ut, closing = closing_pass(s_u, s_w, ring_sums, energy, peers)
    closing = exchange(closing, GROUP)
    grad, loss = grad_pass(
        images, info, closing, rows, own, ring_sums, s_u, s_ut, s_w, energy, lax.axis_size(DP)
    )
    return (loss.reshape(-1), sum_pass(exchange(grad, DP)))


def solution(mesh):
    parts = Mesh(mesh.devices.reshape(4, 4, 2, 4), ("z", "y", "c", "x"))
    return jax.shard_map(
        local,
        mesh=parts,
        in_specs=(P(DP, None), P(DP, None), P(DP, "x"), P(DP, "x"), P(DP), P(DP)),
        out_specs=(P(DP), P(DP, "x")),
        check_vma=False,
    )
```

```python
import functools

import jax
import jax.numpy as jnp
from jax import lax
from jax.experimental import pallas as pl
from jax.experimental.pallas import tpu as pltpu
from jax.sharding import Mesh
from jax.sharding import PartitionSpec as P

PATCH = 256
SWEEPS = 3
EXTRA = 16
LOG2E = 1.4426950408889634
ROWS = 64
SURE = 192
WIDE = 256
PER = 3
HALF = 16
TALL = 32
LANES = 128
SHIFTS = (1, 3, 2)
SIDE = 4
DP = ("z", "y", "c")
GROUP = ("z", "c", "x")

teacher_temp = 0.07
student_temp = 0.1
loss_scale = 65536.0

f32 = jnp.float32
bf16 = jnp.bfloat16

VM = pl.BlockSpec(memory_space=pltpu.VMEM)
SM = pl.BlockSpec(memory_space=pltpu.SMEM)
ANY = pl.BlockSpec(memory_space=pl.ANY)


def params(mib):
    return pltpu.CompilerParams(vmem_limit_bytes=mib * 1024 * 1024)


def pinned(array):
    return pltpu.with_memory_space_constraint(array, pltpu.VMEM)


def shape(dims, dtype=f32):
    return jax.ShapeDtypeStruct(dims, dtype)


def nn(a, b):
    return lax.dot_general(a, b, (((1,), (0,)), ((), ())), preferred_element_type=f32)


def tn(a, b):
    return lax.dot_general(a, b, (((0,), (0,)), ((), ())), preferred_element_type=f32)


def tokens_kernel(me_ref, count_ref, index_ref, teacher_ref, student_ref, *refs):
    tok_out, info_out, feats, sems = refs[-4:]
    copies = [
        pltpu.make_async_copy(ref, feats.at[i], sems.at[i])
        for i, ref in enumerate((teacher_ref, student_ref))
    ]
    for c in copies:
        c.start()
    me = me_ref[0]
    y = (me >> 1) & 3
    info_out[0] = me >> 3
    info_out[1] = me & 1
    info_out[2] = y
    slots = index_ref.shape[0]
    source, d = feats.shape[1:]
    index_row = index_ref[...].reshape(1, slots)
    index_col = jnp.transpose(jnp.broadcast_to(index_row, (8, slots)))[:, 0:1]
    count = count_ref[0]
    live_row = lax.broadcasted_iota(jnp.int32, (1, slots), 1) < count
    live_col = lax.broadcasted_iota(jnp.int32, (slots, 1), 0) < count
    same = ((index_col >> 8) == (index_row >> 8)) & live_col
    own = jnp.sum(jnp.where(same, 1.0, 0.0), axis=0, keepdims=True)
    own = jnp.where(live_row, own, 0.0)
    rest = jnp.concatenate([own[:, d:], jnp.zeros((1, 2 * d - slots), f32)], axis=1)
    at = lax.broadcasted_iota(jnp.int32, (EXTRA, d), 0)
    counts = jnp.where(at == 0, own[:, 0:d], jnp.where(at == 1, rest, 0.0))
    tok_out[slots : slots + EXTRA, :] = counts.astype(bf16)
    pick = jnp.where(
        lax.broadcasted_iota(jnp.int32, (slots, source), 1) == index_col, 1.0, 0.0
    ).astype(bf16)
    to = lax.broadcasted_iota(jnp.int32, (1, d), 1)
    turn = to >> 6
    turn = jnp.where(turn == 2, 3, jnp.where(turn == 3, 2, turn))
    origin = (
        ((to >> 4) & 3) * 64 + ((y + 4 - turn) & 3) * 16 + ((to >> 3) & 1) * 8 + (to & 7)
    )
    order = jnp.where(
        lax.broadcasted_iota(jnp.int32, (d, d), 0) == origin, 1.0, 0.0
    ).astype(bf16)
    for i, at in enumerate((0, slots + EXTRA)):
        copies[i].wait()
        rows = nn(pick, feats[i])
        unit = rows * lax.rsqrt(jnp.sum(rows * rows, axis=1, keepdims=True) + 1e-06)
        tok_out[at : at + slots, :] = nn(unit.astype(bf16), order).astype(bf16)


def tokens(me, count, index, teacher_feat, student_feat, after=()):
    slots, (source, d) = index.shape[0], teacher_feat.shape
    return pl.pallas_call(
        tokens_kernel,
        out_shape=(shape((2 * slots + EXTRA, d), bf16), shape((3,), jnp.int32)),
        in_specs=[SM, SM, VM, ANY, ANY] + [ANY] * len(after),
        out_specs=(VM, SM),
        scratch_shapes=[
            pltpu.VMEM((2, source, d), bf16),
            pltpu.SemaphoreType.DMA((2,)),
        ],
        compiler_params=params(56),
        name="token_rows",
    )(me, count, index, teacher_feat, student_feat, *after)


def weave_kernel(tp_ref, sp_ref, w_out, protos, sems):
    copies = [
        pltpu.make_async_copy(ref, protos.at[i], sems.at[i])
        for i, ref in enumerate((tp_ref, sp_ref))
    ]
    for c in copies:
        c.start()
    for c in copies:
        c.wait()
    parts, _, width = w_out.shape
    for q in range(parts):
        lanes = slice(q * width, (q + 1) * width)
        w_out[q] = jnp.concatenate(
            [protos[0, :, lanes].astype(f32), protos[1, :, lanes].astype(f32)], axis=0
        ).astype(bf16)


def weave(teacher_proto, student_proto):
    rows, cols = teacher_proto.shape
    parts = 8
    return pl.pallas_call(
        weave_kernel,
        out_shape=shape((parts, 2 * rows, cols // parts), bf16),
        in_specs=[ANY, ANY],
        out_specs=VM,
        scratch_shapes=[
            pltpu.VMEM((2, rows, cols), bf16),
            pltpu.SemaphoreType.DMA((2,)),
        ],
        compiler_params=params(56),
        name="weave",
    )(teacher_proto, student_proto)


def stack_kernel(info_ref, *refs):
    toks, (t_out, s_out) = refs[0:4], refs[-2:]
    rows = t_out.shape[1]
    for k, ref in zip((0,) + SHIFTS, toks):
        z = (info_ref[0] + 4 - k) & 3
        t_out[z] = ref[0:rows, :]
        s_out[z] = ref[rows:, :]


def stack(info, toks, slots, after):
    n, d = len(toks), toks[0].shape[1]
    return pl.pallas_call(
        stack_kernel,
        out_shape=(shape((n, slots + EXTRA, d), bf16), shape((n, slots, d), bf16)),
        in_specs=[SM] + [VM] * n + [ANY] * len(after),
        out_specs=(VM, VM),
        compiler_params=params(16),
        name="stack",
    )(info, *toks, *after)


def split_kernel(which, w_ref, *refs):
    out = refs[-1]
    parts, _, width = w_ref.shape
    rows = w_ref[...].astype(f32)[:, 8 * which : 8 * which + 8]
    out[...] = rows.reshape(parts * 8, width).astype(bf16)


def split(which, w, after=()):
    parts, rows, width = w.shape
    return pl.pallas_call(
        functools.partial(split_kernel, which),
        out_shape=shape((parts * rows // 2, width), bf16),
        in_specs=[VM] + [ANY] * len(after),
        out_specs=VM,
        compiler_params=params(16),
        name="split_rows",
    )(w, *after)


def place(info_ref, refs, dst):
    core = info_ref[1]
    for i, ref in enumerate(refs):
        for z in range(ref.shape[0]):
            dst[2 * z + (1 - core if i else core)] = ref[z]


def lay(refs, dst):
    rows = refs[0].shape[0]
    for i, ref in enumerate(refs):
        dst[i * rows : (i + 1) * rows, :] = ref[...]


def inverse_norms(w_ref):
    wide = w_ref[...].astype(f32)
    return lax.rsqrt(jnp.sum(wide * wide, axis=0, keepdims=True) + 1e-06)


def down(rows):
    return jnp.concatenate(
        [
            jnp.transpose(jnp.broadcast_to(rows[j : j + 1, :], (LANES, LANES)))
            for j in range(rows.shape[0])
        ],
        axis=0,
    )


def across(parts_ref):
    return jnp.concatenate(
        [
            jnp.sum(jnp.transpose(parts_ref[j : j + LANES, :]), axis=0, keepdims=True)
            for j in range(0, parts_ref.shape[0], LANES)
        ],
        axis=0,
    )


def vector(ref, b, first=0):
    return ref[pl.ds(first + PER * b, PER), :]


def added(parts_ref):
    total = parts_ref[0].astype(f32)
    for i in range(1, parts_ref.shape[0]):
        total = total + parts_ref[i].astype(f32)
    return total


def live_of(own):
    return jnp.where(own > 0.0, 1.0, 0.0)


def column_factor(refs):
    total = refs[0][...]
    for ref in refs[1:]:
        total = total + ref[...]
    return 1.0 / total


def chunks(n, size):
    return [slice(at, at + size) for at in range(0, n, size)]


def energy_kernel(info_ref, *refs):
    toks, w_refs = refs[0:2], refs[2:6]
    e_ref, own_ref, sum_ref, u, w, live, acc = refs[-7:]
    blocks, slots, cols = e_ref.shape
    place(info_ref, toks, u)
    lay(w_refs, w)
    scale = inverse_norms(w) * (LOG2E / teacher_temp)
    acc[...] = jnp.zeros_like(acc)
    own_ref[...] = jnp.zeros_like(own_ref)

    def step(b, _):
        counts = u[b, slots : slots + EXTRA, :].astype(f32)
        for j in range(PER):
            row, lane = divmod(j * LANES, counts.shape[1])
            own_ref[pl.ds(PER * b + j, 1), :] = counts[row : row + 1, lane : lane + LANES]
        live[...] = down(live_of(vector(own_ref, b)))
        for n in chunks(cols, WIDE):
            raw = nn(u[b, 0:slots, :], w[:, n])
            for i in range(0, WIDE, LANES):
                k = slice(n.start + i, n.start + i + LANES)
                total = acc[:, k]
                for r in chunks(slots, ROWS):
                    energy = jnp.exp2(raw[r, i : i + LANES] * scale[:, k])
                    e_ref[b, r, k] = energy.astype(bf16)
                    total = total + (energy * live[r, :] if r.stop > SURE else energy)
                acc[:, k] = total
        return 0

    lax.fori_loop(0, blocks, step, 0)
    sum_ref[...] = jnp.sum(acc[...], axis=0, keepdims=True)


def energy_pass(info, toks, w_parts, slots, after):
    d, cols = SIDE * w_parts[0].shape[0], w_parts[0].shape[1]
    blocks = 2 * toks[0].shape[0]
    return pl.pallas_call(
        energy_kernel,
        out_shape=(
            pltpu.VMEM((blocks, slots, cols), bf16),
            shape((TALL, LANES)),
            shape((1, cols)),
        ),
        in_specs=[SM] + [VM] * (len(toks) + len(w_parts)) + [ANY] * len(after),
        out_specs=(VM, VM, VM),
        scratch_shapes=[
            pltpu.VMEM((blocks, slots + EXTRA, d), bf16),
            pltpu.VMEM((d, cols), bf16),
            pltpu.VMEM((slots, LANES), f32),
            pltpu.VMEM((ROWS, cols), f32),
        ],
        compiler_params=params(16),
        cost_estimate=pl.CostEstimate(
            flops=2 * blocks * slots * cols * d,
            transcendentals=blocks * slots * cols,
            bytes_accessed=2 * blocks * slots * cols,
        ),
        name="energy_pass",
    )(info, *toks, *w_parts, *after)


def collect_kernel(info_ref, sums_ref, *refs):
    w_refs, toks, (sums_out, w_out, u_out) = refs[0:4], refs[4:6], refs[6:]
    sums_out[...] = sums_ref[...]
    lay(w_refs, w_out)
    place(info_ref, toks, u_out)


def collect(info, sums, w_parts, toks):
    rows, cols = w_parts[0].shape
    n, slots, d = toks[0].shape
    return pl.pallas_call(
        collect_kernel,
        out_shape=(
            shape(sums.shape),
            shape((SIDE * rows, cols), bf16),
            shape((2 * n, slots, d), bf16),
        ),
        in_specs=[SM] + [VM] * (1 + len(w_parts) + len(toks)),
        out_specs=(VM, VM, VM),
        compiler_params=params(16),
        name="collect",
    )(info, sums, *w_parts, *toks)


def row_kernel(*refs):
    sums, e, extra = refs[0:SIDE], refs[SIDE], refs[SIDE + 1 : -3]
    out_ref, part, rows = refs[-3:]
    blocks, slots, cols = e.shape
    c = column_factor(sums)
    rows[...] = jnp.zeros_like(rows)

    def step(b, _):
        for r in chunks(slots, ROWS):
            total = jnp.zeros((ROWS, LANES), f32)
            for k in chunks(cols, LANES):
                total = total + e[b, r, k].astype(f32) * c[:, k]
            part[r, :] = total
        rows[pl.ds(PER * b, PER), :] = across(part)
        return 0

    lax.fori_loop(0, blocks, step, 0)
    at = PER * blocks
    for ref in extra:
        end = at + ref.shape[0]
        if end <= rows.shape[0]:
            rows[at:end, :] = ref[...]
        at = end
    low = rows[...].astype(bf16)
    for i in range(out_ref.shape[0]):
        out_ref[i] = low


def row_pass(sums, energy, peers, tall, extra):
    blocks, slots, cols = energy.shape
    return pl.pallas_call(
        row_kernel,
        out_shape=shape((peers, tall, LANES), bf16),
        in_specs=[VM] * (SIDE + 1 + len(extra)),
        out_specs=VM,
        scratch_shapes=[pltpu.VMEM((slots, LANES), f32), pltpu.VMEM((tall, LANES), f32)],
        compiler_params=params(8),
        name="row_pass",
    )(*sums, pinned(energy), *extra)


def column_kernel(rows_ref, own_ref, e, out_ref, weight, ratio, acc):
    blocks, slots, cols = e.shape
    acc[...] = jnp.zeros_like(acc)
    own = own_ref[...]
    total = added(rows_ref)[0 : own.shape[0]]
    ratio[...] = live_of(own) / jnp.where(own > 0.0, total, 1.0)

    def step(b, _):
        weight[...] = down(vector(ratio, b))
        for k in chunks(cols, LANES):
            total = acc[:, k]
            for r in chunks(slots, ROWS):
                total = total + e[b, r, k].astype(f32) * weight[r, :]
            acc[:, k] = total
        return 0

    lax.fori_loop(0, blocks, step, 0)
    out_ref[...] = jnp.sum(acc[...], axis=0, keepdims=True)


def column_pass(rows, own, energy):
    blocks, slots, cols = energy.shape
    return pl.pallas_call(
        column_kernel,
        out_shape=shape((1, cols)),
        in_specs=[VM, VM, VM],
        out_specs=VM,
        scratch_shapes=[
            pltpu.VMEM((slots, LANES), f32),
            pltpu.VMEM((TALL, LANES), f32),
            pltpu.VMEM((ROWS, cols), f32),
        ],
        compiler_params=params(8),
        name="column_pass",
    )(rows, own, pinned(energy))


def softmax_kernel(first, u, w, out_ref, part):
    _, slots, _ = u.shape
    cols = w.shape[1]
    scale = inverse_norms(w) * (LOG2E / student_temp)

    def step(b, _):
        part[...] = jnp.zeros_like(part)
        for n in chunks(cols, cols // 2):
            raw = nn(u[first + b], w[:, n])
            for r in chunks(slots, ROWS):
                total = part[r, :]
                for i in range(0, cols // 2, LANES):
                    k = slice(n.start + i, n.start + i + LANES)
                    total = total + jnp.exp2(raw[r, i : i + LANES] * scale[:, k])
                part[r, :] = total
        out_ref[pl.ds(PER * b, PER), :] = across(part)
        return 0

    lax.fori_loop(0, out_ref.shape[0] // PER, step, 0)


def softmax_pass(u, w, first, count):
    blocks, slots, d = u.shape
    cols = w.shape[1]
    return pl.pallas_call(
        functools.partial(softmax_kernel, first),
        out_shape=shape((PER * count, LANES)),
        in_specs=[VM, VM],
        out_specs=VM,
        scratch_shapes=[pltpu.VMEM((slots, LANES), f32)],
        compiler_params=params(16),
        cost_estimate=pl.CostEstimate(
            flops=2 * count * slots * cols * d,
            transcendentals=count * slots * cols,
            bytes_accessed=count * slots * d,
        ),
        name="softmax_pass",
    )(u, w)


def closing_kernel(u, w, *refs):
    sums, (e, ut, out_ref, part, rows, crosses) = refs[0:SIDE], refs[SIDE:]
    blocks, slots, cols = e.shape
    c = column_factor(sums)
    cs = c * (inverse_norms(w) * (1.0 / student_temp))
    rows[...] = jnp.zeros_like(rows)

    def step(b, _):
        ut[b] = jnp.transpose(u[b].astype(f32)).astype(bf16)
        part[...] = jnp.zeros_like(part)
        for n in chunks(cols, cols // 2):
            raw = nn(u[b], w[:, n])
            for r in chunks(slots, ROWS):
                mass, cross = part[0, r, :], part[1, r, :]
                for i in range(0, cols // 2, LANES):
                    k = slice(n.start + i, n.start + i + LANES)
                    energy = e[b, r, k].astype(f32)
                    mass = mass + energy * c[:, k]
                    cross = cross + energy * cs[:, k] * raw[r, i : i + LANES]
                part[0, r, :], part[1, r, :] = mass, cross
        rows[pl.ds(PER * b, PER), :] = across(part.at[0])
        crosses[b, 0:PER, :] = across(part.at[1])
        return 0

    lax.fori_loop(0, blocks, step, 0)
    at = PER * blocks
    for i in range(out_ref.shape[0]):
        rows[at : at + PER, :] = crosses[i // 4, 0:PER, :]
        out_ref[i] = rows[...].astype(bf16)


def closing_pass(u, w, sums, energy, peers):
    blocks, slots, cols = energy.shape
    d = w.shape[0]
    return pl.pallas_call(
        closing_kernel,
        out_shape=(
            pltpu.VMEM((blocks, d, slots), bf16),
            shape((peers, TALL, LANES), bf16),
        ),
        in_specs=[VM] * (SIDE + 3),
        out_specs=(VM, VM),
        scratch_shapes=[
            pltpu.VMEM((2, slots, LANES), f32),
            pltpu.VMEM((TALL, LANES), f32),
            pltpu.VMEM((blocks, 8, LANES), f32),
        ],
        compiler_params=params(16),
        name="closing_pass",
    )(u, w, *sums, pinned(energy))


def grad_kernel(images, info_ref, rows_ref, softs_ref, own_ref, *refs):
    sums = refs[0:SIDE]
    (u, ut, w, e, out_ref, loss_ref, soft_w, mass_w, acc, totals, soft_all,
     mass_all) = refs[SIDE:]
    blocks, slots, cols = e.shape
    totals[...] = added(rows_ref)
    own = own_ref[...]
    n = PER * blocks
    me = info_ref[0] * 2 + info_ref[1]
    soft_all[0:n, :] = added(softs_ref)[n : 2 * n]
    mine = jnp.log(vector(soft_all, me)) - vector(totals, 0, n) / vector(totals, me)
    loss_ref[...] = jnp.where(vector(own_ref, me) > 0.0, mine, 0.0)
    weight = live_of(own) / (jnp.maximum(own, 1.0) * images) * (loss_scale / student_temp)
    soft_all[0:n, :] = weight[0:n] / soft_all[0:n, :]
    mass_all[0:n, :] = weight[0:n] / totals[0:n, :]
    c = column_factor(sums)
    inv = inverse_norms(w)
    scale = inv * (LOG2E / student_temp)
    acc[...] = jnp.zeros_like(acc)

    def step(s, _):
        for half in range(2):
            at = slice(half * slots, (half + 1) * slots)
            soft_w[at, :] = down(vector(soft_all, 2 * s + half))
            mass_w[at, :] = down(vector(mass_all, 2 * s + half))
        units = jnp.concatenate([ut[2 * s], ut[2 * s + 1]], axis=1)
        for n in chunks(cols, WIDE):
            raws = [nn(u[2 * s + half], w[:, n]) for half in range(2)]
            parts = []
            for half in range(2):
                b = 2 * s + half
                for r in chunks(slots, ROWS):
                    at = slice(half * slots + r.start, half * slots + r.stop)
                    soft_r, mass_r = soft_w[at, :], mass_w[at, :]
                    line = []
                    for i in range(0, WIDE, LANES):
                        k = slice(n.start + i, n.start + i + LANES)
                        power = raws[half][r, i : i + LANES] * scale[:, k]
                        target = e[b, r, k].astype(f32) * c[:, k] * mass_r
                        line.append((jnp.exp2(power) * soft_r - target).astype(bf16))
                    parts.append(jnp.concatenate(line, axis=1))
            acc[:, n] += nn(units, jnp.concatenate(parts, axis=0))
        return 0

    lax.fori_loop(0, blocks // 2, step, 0)
    grad = acc[...]
    unit = w[...].astype(f32) * inv
    dot = jnp.sum(grad * unit, axis=0, keepdims=True)
    acc[...] = inv * (grad - unit * dot)
    rows = out_ref.shape[1]
    for i, k in enumerate((0,) + SHIFTS):
        y = (info_ref[2] + 4 - k) & 3
        for q in range(8):
            at = (8 * i + q) * rows
            out_ref[(q // 2) * 8 + 2 * y + q % 2] = acc[at : at + rows, :].astype(bf16)


def grad_pass(images, info, rows, softs, own, sums, u, ut, w, energy, peers):
    blocks, slots, cols = energy.shape
    d = ut.shape[1]
    return pl.pallas_call(
        functools.partial(grad_kernel, float(images)),
        out_shape=(shape((peers, d // peers, cols), bf16), shape((PER, LANES))),
        in_specs=[SM] + [VM] * (SIDE + 7),
        out_specs=(VM, VM),
        scratch_shapes=[
            pltpu.VMEM((2 * slots, LANES), f32),
            pltpu.VMEM((2 * slots, LANES), f32),
            pltpu.VMEM((d, cols), f32),
            pltpu.VMEM((TALL, LANES), f32),
            pltpu.VMEM((TALL, LANES), f32),
            pltpu.VMEM((TALL, LANES), f32),
        ],
        compiler_params=params(16),
        name="grad_pass",
    )(info, rows, softs, own, *sums, u, ut, w, pinned(energy))


def sum_kernel(parts_ref, out_ref):
    peers, _, width = parts_ref.shape
    for q in range(peers // SIDE):
        first = (q // 2) * 2 * SIDE + q % 2
        total = parts_ref[first].astype(f32)
        for y in range(1, SIDE):
            total = total + parts_ref[first + 2 * y].astype(f32)
        out_ref[:, q * width : (q + 1) * width] = total


def sum_pass(parts):
    peers, rows, width = parts.shape
    return pl.pallas_call(
        sum_kernel,
        out_shape=shape((rows, peers // SIDE * width)),
        in_specs=[VM],
        out_specs=VM,
        compiler_params=params(16),
        name="sum_pass",
    )(parts)


def shift(value, axis, k):
    n = lax.axis_size(axis)
    return lax.ppermute(value, axis, [(i, (i + k) % n) for i in range(n)])


def exchange(value, axes):
    return lax.all_to_all(value, axes, 0, 0, tiled=True)


def ring(value, axis):
    return [value] + [shift(value, axis, k) for k in SHIFTS]


def local(teacher_feat, student_feat, teacher_proto, student_proto, mask_index, mask_count):
    slots = mask_index.shape[0]
    images = lax.axis_size(DP) * (teacher_feat.shape[0] // PATCH)
    peers = lax.axis_size(GROUP)
    me = lax.axis_index(DP).reshape(1)
    w = weave(teacher_proto, student_proto)
    tok, info = tokens(me, mask_count, mask_index, teacher_feat, student_feat)
    w = exchange(w, ("z", "c"))
    t_parts = ring(split(0, w), "y")
    t_mine, s_mine = stack(info, ring(tok, "z"), slots, t_parts[1:])
    t_toks, s_toks = ([v, shift(v, "c", 1)] for v in (t_mine, s_mine))
    s_parts = ring(split(1, w, t_parts[1:]), "y")
    energy, own, sums = energy_pass(info, t_toks, t_parts, slots, s_parts[:1])
    sums, s_w, s_u = collect(info, sums, s_parts, s_toks)
    half = s_u.shape[0] // 2
    soft = []
    for i in range(SWEEPS - 1):
        soft.append(softmax_pass(s_u, s_w, half * i, half))
        tall = TALL if i < SWEEPS - 2 else TALL + HALF
        rows = exchange(row_pass(ring(sums, "y"), energy, peers, tall, soft), GROUP)
        sums = column_pass(rows, own, energy)
    ring_sums = ring(sums, "y")
    s_ut, closing = closing_pass(s_u, s_w, ring_sums, energy, peers)
    closing = exchange(closing, GROUP)
    grad, loss = grad_pass(
        images, info, closing, rows, own, ring_sums, s_u, s_ut, s_w, energy, lax.axis_size(DP)
    )
    return (loss.reshape(-1), sum_pass(exchange(grad, DP)))


def solution(mesh):
    parts = Mesh(mesh.devices.reshape(4, 4, 2, 4), ("z", "y", "c", "x"))
    return jax.shard_map(
        local,
        mesh=parts,
        in_specs=(P(DP, None), P(DP, None), P(DP, "x"), P(DP, "x"), P(DP), P(DP)),
        out_specs=(P(DP), P(DP, "x")),
        check_vma=False,
    )
```

```python
import functools

import jax
import jax.numpy as jnp
from jax import lax
from jax.experimental import pallas as pl
from jax.experimental.pallas import tpu as pltpu
from jax.sharding import Mesh
from jax.sharding import PartitionSpec as P

PATCH = 256
SWEEPS = 3
EXTRA = 16
LOG2E = 1.4426950408889634
ROWS = 64
SURE = 192
WIDE = 256
PER = 3
HALF = 16
TALL = 32
LANES = 128
SHIFTS = (1, 3, 2)
SIDE = 4
DP = ("z", "y", "c")
GROUP = ("x", "z", "c")

teacher_temp = 0.07
student_temp = 0.1
loss_scale = 65536.0

f32 = jnp.float32
bf16 = jnp.bfloat16

VM = pl.BlockSpec(memory_space=pltpu.VMEM)
SM = pl.BlockSpec(memory_space=pltpu.SMEM)
ANY = pl.BlockSpec(memory_space=pl.ANY)


def params(mib):
    return pltpu.CompilerParams(vmem_limit_bytes=mib * 1024 * 1024)


def pinned(array):
    return pltpu.with_memory_space_constraint(array, pltpu.VMEM)


def shape(dims, dtype=f32):
    return jax.ShapeDtypeStruct(dims, dtype)


def nn(a, b):
    return lax.dot_general(a, b, (((1,), (0,)), ((), ())), preferred_element_type=f32)


def tn(a, b):
    return lax.dot_general(a, b, (((0,), (0,)), ((), ())), preferred_element_type=f32)


def tokens_kernel(me_ref, count_ref, index_ref, teacher_ref, student_ref, *refs):
    tok_out, info_out, feats, sems = refs[-4:]
    copies = [
        pltpu.make_async_copy(ref, feats.at[i], sems.at[i])
        for i, ref in enumerate((teacher_ref, student_ref))
    ]
    for c in copies:
        c.start()
    me = me_ref[0]
    y = (me >> 1) & 3
    info_out[0] = me >> 3
    info_out[1] = me & 1
    info_out[2] = y
    slots = index_ref.shape[0]
    source, d = feats.shape[1:]
    index_row = index_ref[...].reshape(1, slots)
    index_col = jnp.transpose(jnp.broadcast_to(index_row, (8, slots)))[:, 0:1]
    count = count_ref[0]
    live_row = lax.broadcasted_iota(jnp.int32, (1, slots), 1) < count
    live_col = lax.broadcasted_iota(jnp.int32, (slots, 1), 0) < count
    same = ((index_col >> 8) == (index_row >> 8)) & live_col
    own = jnp.sum(jnp.where(same, 1.0, 0.0), axis=0, keepdims=True)
    own = jnp.where(live_row, own, 0.0)
    rest = jnp.concatenate([own[:, d:], jnp.zeros((1, 2 * d - slots), f32)], axis=1)
    at = lax.broadcasted_iota(jnp.int32, (EXTRA, d), 0)
    counts = jnp.where(at == 0, own[:, 0:d], jnp.where(at == 1, rest, 0.0))
    tok_out[slots : slots + EXTRA, :] = counts.astype(bf16)
    pick = jnp.where(
        lax.broadcasted_iota(jnp.int32, (slots, source), 1) == index_col, 1.0, 0.0
    ).astype(bf16)
    to = lax.broadcasted_iota(jnp.int32, (1, d), 1)
    turn = to >> 6
    turn = jnp.where(turn == 2, 3, jnp.where(turn == 3, 2, turn))
    origin = (
        ((to >> 4) & 3) * 64 + ((y + 4 - turn) & 3) * 16 + ((to >> 3) & 1) * 8 + (to & 7)
    )
    order = jnp.where(
        lax.broadcasted_iota(jnp.int32, (d, d), 0) == origin, 1.0, 0.0
    ).astype(bf16)
    for i, at in enumerate((0, slots + EXTRA)):
        copies[i].wait()
        rows = nn(pick, feats[i])
        unit = rows * lax.rsqrt(jnp.sum(rows * rows, axis=1, keepdims=True) + 1e-06)
        tok_out[at : at + slots, :] = nn(unit.astype(bf16), order).astype(bf16)


def tokens(me, count, index, teacher_feat, student_feat, after=()):
    slots, (source, d) = index.shape[0], teacher_feat.shape
    return pl.pallas_call(
        tokens_kernel,
        out_shape=(shape((2 * slots + EXTRA, d), bf16), shape((3,), jnp.int32)),
        in_specs=[SM, SM, VM, ANY, ANY] + [ANY] * len(after),
        out_specs=(VM, SM),
        scratch_shapes=[
            pltpu.VMEM((2, source, d), bf16),
            pltpu.SemaphoreType.DMA((2,)),
        ],
        compiler_params=params(56),
        name="token_rows",
    )(me, count, index, teacher_feat, student_feat, *after)


def weave_kernel(tp_ref, sp_ref, w_out, protos, sems):
    copies = [
        pltpu.make_async_copy(ref, protos.at[i], sems.at[i])
        for i, ref in enumerate((tp_ref, sp_ref))
    ]
    for c in copies:
        c.start()
    for c in copies:
        c.wait()
    parts, _, width = w_out.shape
    for q in range(parts):
        lanes = slice(q * width, (q + 1) * width)
        w_out[q] = jnp.concatenate(
            [protos[0, :, lanes].astype(f32), protos[1, :, lanes].astype(f32)], axis=0
        ).astype(bf16)


def weave(teacher_proto, student_proto):
    rows, cols = teacher_proto.shape
    parts = 8
    return pl.pallas_call(
        weave_kernel,
        out_shape=shape((parts, 2 * rows, cols // parts), bf16),
        in_specs=[ANY, ANY],
        out_specs=VM,
        scratch_shapes=[
            pltpu.VMEM((2, rows, cols), bf16),
            pltpu.SemaphoreType.DMA((2,)),
        ],
        compiler_params=params(56),
        name="weave",
    )(teacher_proto, student_proto)


def stack_kernel(info_ref, *refs):
    toks, (t_out, s_out) = refs[0:4], refs[-2:]
    rows = t_out.shape[1]
    for k, ref in zip((0,) + SHIFTS, toks):
        z = (info_ref[0] + 4 - k) & 3
        t_out[z] = ref[0:rows, :]
        s_out[z] = ref[rows:, :]


def stack(info, toks, slots, after):
    n, d = len(toks), toks[0].shape[1]
    return pl.pallas_call(
        stack_kernel,
        out_shape=(shape((n, slots + EXTRA, d), bf16), shape((n, slots, d), bf16)),
        in_specs=[SM] + [VM] * n + [ANY] * len(after),
        out_specs=(VM, VM),
        compiler_params=params(16),
        name="stack",
    )(info, *toks, *after)


def split_kernel(which, w_ref, *refs):
    out = refs[-1]
    parts, _, width = w_ref.shape
    rows = w_ref[...].astype(f32)[:, 8 * which : 8 * which + 8]
    out[...] = rows.reshape(parts * 8, width).astype(bf16)


def split(which, w, after=()):
    parts, rows, width = w.shape
    return pl.pallas_call(
        functools.partial(split_kernel, which),
        out_shape=shape((parts * rows // 2, width), bf16),
        in_specs=[VM] + [ANY] * len(after),
        out_specs=VM,
        compiler_params=params(16),
        name="split_rows",
    )(w, *after)


def place(info_ref, refs, dst):
    core = info_ref[1]
    for i, ref in enumerate(refs):
        for z in range(ref.shape[0]):
            dst[2 * z + (1 - core if i else core)] = ref[z]


def lay(refs, dst):
    rows = refs[0].shape[0]
    for i, ref in enumerate(refs):
        dst[i * rows : (i + 1) * rows, :] = ref[...]


def inverse_norms(w_ref):
    wide = w_ref[...].astype(f32)
    return lax.rsqrt(jnp.sum(wide * wide, axis=0, keepdims=True) + 1e-06)


def down(rows):
    return jnp.concatenate(
        [
            jnp.transpose(jnp.broadcast_to(rows[j : j + 1, :], (LANES, LANES)))
            for j in range(rows.shape[0])
        ],
        axis=0,
    )


def across(parts_ref):
    return jnp.concatenate(
        [
            jnp.sum(jnp.transpose(parts_ref[j : j + LANES, :]), axis=0, keepdims=True)
            for j in range(0, parts_ref.shape[0], LANES)
        ],
        axis=0,
    )


def vector(ref, b, first=0):
    return ref[pl.ds(first + PER * b, PER), :]


def added(parts_ref):
    total = parts_ref[0].astype(f32)
    for i in range(1, parts_ref.shape[0]):
        total = total + parts_ref[i].astype(f32)
    return total


def live_of(own):
    return jnp.where(own > 0.0, 1.0, 0.0)


def column_factor(refs):
    total = refs[0][...]
    for ref in refs[1:]:
        total = total + ref[...]
    return 1.0 / total


def chunks(n, size):
    return [slice(at, at + size) for at in range(0, n, size)]


def energy_kernel(info_ref, *refs):
    toks, w_refs = refs[0:2], refs[2:6]
    e_ref, own_ref, sum_ref, u, w, live, acc = refs[-7:]
    blocks, slots, cols = e_ref.shape
    place(info_ref, toks, u)
    lay(w_refs, w)
    scale = inverse_norms(w) * (LOG2E / teacher_temp)
    acc[...] = jnp.zeros_like(acc)
    own_ref[...] = jnp.zeros_like(own_ref)

    def step(b, _):
        counts = u[b, slots : slots + EXTRA, :].astype(f32)
        for j in range(PER):
            row, lane = divmod(j * LANES, counts.shape[1])
            own_ref[pl.ds(PER * b + j, 1), :] = counts[row : row + 1, lane : lane + LANES]
        live[...] = down(live_of(vector(own_ref, b)))
        for n in chunks(cols, WIDE):
            raw = nn(u[b, 0:slots, :], w[:, n])
            for i in range(0, WIDE, LANES):
                k = slice(n.start + i, n.start + i + LANES)
                total = acc[:, k]
                for r in chunks(slots, ROWS):
                    energy = jnp.exp2(raw[r, i : i + LANES] * scale[:, k])
                    e_ref[b, r, k] = energy.astype(bf16)
                    total = total + (energy * live[r, :] if r.stop > SURE else energy)
                acc[:, k] = total
        return 0

    lax.fori_loop(0, blocks, step, 0)
    sum_ref[...] = jnp.sum(acc[...], axis=0, keepdims=True)


def energy_pass(info, toks, w_parts, slots, after):
    d, cols = SIDE * w_parts[0].shape[0], w_parts[0].shape[1]
    blocks = 2 * toks[0].shape[0]
    return pl.pallas_call(
        energy_kernel,
        out_shape=(
            pltpu.VMEM((blocks, slots, cols), bf16),
            shape((TALL, LANES)),
            shape((1, cols)),
        ),
        in_specs=[SM] + [VM] * (len(toks) + len(w_parts)) + [ANY] * len(after),
        out_specs=(VM, VM, VM),
        scratch_shapes=[
            pltpu.VMEM((blocks, slots + EXTRA, d), bf16),
            pltpu.VMEM((d, cols), bf16),
            pltpu.VMEM((slots, LANES), f32),
            pltpu.VMEM((ROWS, cols), f32),
        ],
        compiler_params=params(16),
        cost_estimate=pl.CostEstimate(
            flops=2 * blocks * slots * cols * d,
            transcendentals=blocks * slots * cols,
            bytes_accessed=2 * blocks * slots * cols,
        ),
        name="energy_pass",
    )(info, *toks, *w_parts, *after)


def collect_kernel(info_ref, sums_ref, *refs):
    w_refs, toks, (sums_out, w_out, u_out) = refs[0:4], refs[4:6], refs[6:]
    sums_out[...] = sums_ref[...]
    lay(w_refs, w_out)
    place(info_ref, toks, u_out)


def collect(info, sums, w_parts, toks):
    rows, cols = w_parts[0].shape
    n, slots, d = toks[0].shape
    return pl.pallas_call(
        collect_kernel,
        out_shape=(
            shape(sums.shape),
            shape((SIDE * rows, cols), bf16),
            shape((2 * n, slots, d), bf16),
        ),
        in_specs=[SM] + [VM] * (1 + len(w_parts) + len(toks)),
        out_specs=(VM, VM, VM),
        compiler_params=params(16),
        name="collect",
    )(info, sums, *w_parts, *toks)


def row_kernel(*refs):
    sums, e, extra = refs[0:SIDE], refs[SIDE], refs[SIDE + 1 : -3]
    out_ref, part, rows = refs[-3:]
    blocks, slots, cols = e.shape
    c = column_factor(sums)
    rows[...] = jnp.zeros_like(rows)

    def step(b, _):
        for r in chunks(slots, ROWS):
            total = jnp.zeros((ROWS, LANES), f32)
            for k in chunks(cols, LANES):
                total = total + e[b, r, k].astype(f32) * c[:, k]
            part[r, :] = total
        rows[pl.ds(PER * b, PER), :] = across(part)
        return 0

    lax.fori_loop(0, blocks, step, 0)
    at = PER * blocks
    for ref in extra:
        end = at + ref.shape[0]
        if end <= rows.shape[0]:
            rows[at:end, :] = ref[...]
        at = end
    low = rows[...].astype(bf16)
    for i in range(out_ref.shape[0]):
        out_ref[i] = low


def row_pass(sums, energy, peers, tall, extra):
    blocks, slots, cols = energy.shape
    return pl.pallas_call(
        row_kernel,
        out_shape=shape((peers, tall, LANES), bf16),
        in_specs=[VM] * (SIDE + 1 + len(extra)),
        out_specs=VM,
        scratch_shapes=[pltpu.VMEM((slots, LANES), f32), pltpu.VMEM((tall, LANES), f32)],
        compiler_params=params(8),
        name="row_pass",
    )(*sums, pinned(energy), *extra)


def column_kernel(rows_ref, own_ref, e, out_ref, weight, ratio, acc):
    blocks, slots, cols = e.shape
    acc[...] = jnp.zeros_like(acc)
    own = own_ref[...]
    total = added(rows_ref)[0 : own.shape[0]]
    ratio[...] = live_of(own) / jnp.where(own > 0.0, total, 1.0)

    def step(b, _):
        weight[...] = down(vector(ratio, b))
        for k in chunks(cols, LANES):
            total = acc[:, k]
            for r in chunks(slots, ROWS):
                total = total + e[b, r, k].astype(f32) * weight[r, :]
            acc[:, k] = total
        return 0

    lax.fori_loop(0, blocks, step, 0)
    out_ref[...] = jnp.sum(acc[...], axis=0, keepdims=True)


def column_pass(rows, own, energy):
    blocks, slots, cols = energy.shape
    return pl.pallas_call(
        column_kernel,
        out_shape=shape((1, cols)),
        in_specs=[VM, VM, VM],
        out_specs=VM,
        scratch_shapes=[
            pltpu.VMEM((slots, LANES), f32),
            pltpu.VMEM((TALL, LANES), f32),
            pltpu.VMEM((ROWS, cols), f32),
        ],
        compiler_params=params(8),
        name="column_pass",
    )(rows, own, pinned(energy))


def softmax_kernel(first, u, w, out_ref, part):
    _, slots, _ = u.shape
    cols = w.shape[1]
    scale = inverse_norms(w) * (LOG2E / student_temp)

    def step(b, _):
        part[...] = jnp.zeros_like(part)
        for n in chunks(cols, cols // 2):
            raw = nn(u[first + b], w[:, n])
            for r in chunks(slots, ROWS):
                total = part[r, :]
                for i in range(0, cols // 2, LANES):
                    k = slice(n.start + i, n.start + i + LANES)
                    total = total + jnp.exp2(raw[r, i : i + LANES] * scale[:, k])
                part[r, :] = total
        out_ref[pl.ds(PER * b, PER), :] = across(part)
        return 0

    lax.fori_loop(0, out_ref.shape[0] // PER, step, 0)


def softmax_pass(u, w, first, count):
    blocks, slots, d = u.shape
    cols = w.shape[1]
    return pl.pallas_call(
        functools.partial(softmax_kernel, first),
        out_shape=shape((PER * count, LANES)),
        in_specs=[VM, VM],
        out_specs=VM,
        scratch_shapes=[pltpu.VMEM((slots, LANES), f32)],
        compiler_params=params(16),
        cost_estimate=pl.CostEstimate(
            flops=2 * count * slots * cols * d,
            transcendentals=count * slots * cols,
            bytes_accessed=count * slots * d,
        ),
        name="softmax_pass",
    )(u, w)


def closing_kernel(u, w, *refs):
    sums, (e, ut, out_ref, part, rows, crosses) = refs[0:SIDE], refs[SIDE:]
    blocks, slots, cols = e.shape
    c = column_factor(sums)
    cs = c * (inverse_norms(w) * (1.0 / student_temp))
    rows[...] = jnp.zeros_like(rows)

    def step(b, _):
        ut[b] = jnp.transpose(u[b].astype(f32)).astype(bf16)
        part[...] = jnp.zeros_like(part)
        for n in chunks(cols, cols // 2):
            raw = nn(u[b], w[:, n])
            for r in chunks(slots, ROWS):
                mass, cross = part[0, r, :], part[1, r, :]
                for i in range(0, cols // 2, LANES):
                    k = slice(n.start + i, n.start + i + LANES)
                    energy = e[b, r, k].astype(f32)
                    mass = mass + energy * c[:, k]
                    cross = cross + energy * cs[:, k] * raw[r, i : i + LANES]
                part[0, r, :], part[1, r, :] = mass, cross
        rows[pl.ds(PER * b, PER), :] = across(part.at[0])
        crosses[b, 0:PER, :] = across(part.at[1])
        return 0

    lax.fori_loop(0, blocks, step, 0)
    at = PER * blocks
    for i in range(out_ref.shape[0]):
        rows[at : at + PER, :] = crosses[i % 8, 0:PER, :]
        out_ref[i] = rows[...].astype(bf16)


def closing_pass(u, w, sums, energy, peers):
    blocks, slots, cols = energy.shape
    d = w.shape[0]
    return pl.pallas_call(
        closing_kernel,
        out_shape=(
            pltpu.VMEM((blocks, d, slots), bf16),
            shape((peers, TALL, LANES), bf16),
        ),
        in_specs=[VM] * (SIDE + 3),
        out_specs=(VM, VM),
        scratch_shapes=[
            pltpu.VMEM((2, slots, LANES), f32),
            pltpu.VMEM((TALL, LANES), f32),
            pltpu.VMEM((blocks, 8, LANES), f32),
        ],
        compiler_params=params(16),
        name="closing_pass",
    )(u, w, *sums, pinned(energy))


def grad_kernel(images, info_ref, rows_ref, softs_ref, own_ref, *refs):
    sums = refs[0:SIDE]
    (u, ut, w, e, out_ref, loss_ref, soft_w, mass_w, acc, totals, soft_all,
     mass_all) = refs[SIDE:]
    blocks, slots, cols = e.shape
    totals[...] = added(rows_ref)
    own = own_ref[...]
    n = PER * blocks
    me = info_ref[0] * 2 + info_ref[1]
    soft_all[0:n, :] = added(softs_ref)[n : 2 * n]
    mine = jnp.log(vector(soft_all, me)) - vector(totals, 0, n) / vector(totals, me)
    loss_ref[...] = jnp.where(vector(own_ref, me) > 0.0, mine, 0.0)
    weight = live_of(own) / (jnp.maximum(own, 1.0) * images) * (loss_scale / student_temp)
    soft_all[0:n, :] = weight[0:n] / soft_all[0:n, :]
    mass_all[0:n, :] = weight[0:n] / totals[0:n, :]
    c = column_factor(sums)
    inv = inverse_norms(w)
    scale = inv * (LOG2E / student_temp)
    acc[...] = jnp.zeros_like(acc)

    def step(s, _):
        for half in range(2):
            at = slice(half * slots, (half + 1) * slots)
            soft_w[at, :] = down(vector(soft_all, 2 * s + half))
            mass_w[at, :] = down(vector(mass_all, 2 * s + half))
        units = jnp.concatenate([ut[2 * s], ut[2 * s + 1]], axis=1)
        for n in chunks(cols, WIDE):
            raws = [nn(u[2 * s + half], w[:, n]) for half in range(2)]
            parts = []
            for half in range(2):
                b = 2 * s + half
                for r in chunks(slots, ROWS):
                    at = slice(half * slots + r.start, half * slots + r.stop)
                    soft_r, mass_r = soft_w[at, :], mass_w[at, :]
                    line = []
                    for i in range(0, WIDE, LANES):
                        k = slice(n.start + i, n.start + i + LANES)
                        power = raws[half][r, i : i + LANES] * scale[:, k]
                        target = e[b, r, k].astype(f32) * c[:, k] * mass_r
                        line.append((jnp.exp2(power) * soft_r - target).astype(bf16))
                    parts.append(jnp.concatenate(line, axis=1))
            acc[:, n] += nn(units, jnp.concatenate(parts, axis=0))
        return 0

    lax.fori_loop(0, blocks // 2, step, 0)
    grad = acc[...]
    unit = w[...].astype(f32) * inv
    dot = jnp.sum(grad * unit, axis=0, keepdims=True)
    acc[...] = inv * (grad - unit * dot)
    rows = out_ref.shape[1]
    for i, k in enumerate((0,) + SHIFTS):
        y = (info_ref[2] + 4 - k) & 3
        for q in range(8):
            at = (8 * i + q) * rows
            out_ref[(q // 2) * 8 + 2 * y + q % 2] = acc[at : at + rows, :].astype(bf16)


def grad_pass(images, info, rows, softs, own, sums, u, ut, w, energy, peers):
    blocks, slots, cols = energy.shape
    d = ut.shape[1]
    return pl.pallas_call(
        functools.partial(grad_kernel, float(images)),
        out_shape=(shape((peers, d // peers, cols), bf16), shape((PER, LANES))),
        in_specs=[SM] + [VM] * (SIDE + 7),
        out_specs=(VM, VM),
        scratch_shapes=[
            pltpu.VMEM((2 * slots, LANES), f32),
            pltpu.VMEM((2 * slots, LANES), f32),
            pltpu.VMEM((d, cols), f32),
            pltpu.VMEM((TALL, LANES), f32),
            pltpu.VMEM((TALL, LANES), f32),
            pltpu.VMEM((TALL, LANES), f32),
        ],
        compiler_params=params(16),
        name="grad_pass",
    )(info, rows, softs, own, *sums, u, ut, w, pinned(energy))


def sum_kernel(parts_ref, out_ref):
    peers, _, width = parts_ref.shape
    for q in range(peers // SIDE):
        first = (q // 2) * 2 * SIDE + q % 2
        total = parts_ref[first].astype(f32)
        for y in range(1, SIDE):
            total = total + parts_ref[first + 2 * y].astype(f32)
        out_ref[:, q * width : (q + 1) * width] = total


def sum_pass(parts):
    peers, rows, width = parts.shape
    return pl.pallas_call(
        sum_kernel,
        out_shape=shape((rows, peers // SIDE * width)),
        in_specs=[VM],
        out_specs=VM,
        compiler_params=params(16),
        name="sum_pass",
    )(parts)


def shift(value, axis, k):
    n = lax.axis_size(axis)
    return lax.ppermute(value, axis, [(i, (i + k) % n) for i in range(n)])


def exchange(value, axes):
    return lax.all_to_all(value, axes, 0, 0, tiled=True)


def ring(value, axis):
    return [value] + [shift(value, axis, k) for k in SHIFTS]


def local(teacher_feat, student_feat, teacher_proto, student_proto, mask_index, mask_count):
    slots = mask_index.shape[0]
    images = lax.axis_size(DP) * (teacher_feat.shape[0] // PATCH)
    peers = lax.axis_size(GROUP)
    me = lax.axis_index(DP).reshape(1)
    w = weave(teacher_proto, student_proto)
    tok, info = tokens(me, mask_count, mask_index, teacher_feat, student_feat)
    w = exchange(w, ("z", "c"))
    t_parts = ring(split(0, w), "y")
    t_mine, s_mine = stack(info, ring(tok, "z"), slots, t_parts[1:])
    t_toks, s_toks = ([v, shift(v, "c", 1)] for v in (t_mine, s_mine))
    s_parts = ring(split(1, w, t_parts[1:]), "y")
    energy, own, sums = energy_pass(info, t_toks, t_parts, slots, s_parts[:1])
    sums, s_w, s_u = collect(info, sums, s_parts, s_toks)
    half = s_u.shape[0] // 2
    soft = []
    for i in range(SWEEPS - 1):
        soft.append(softmax_pass(s_u, s_w, half * i, half))
        tall = TALL if i < SWEEPS - 2 else TALL + HALF
        rows = exchange(row_pass(ring(sums, "y"), energy, peers, tall, soft), GROUP)
        sums = column_pass(rows, own, energy)
    ring_sums = ring(sums, "y")
    s_ut, closing = closing_pass(s_u, s_w, ring_sums, energy, peers)
    closing = exchange(closing, GROUP)
    grad, loss = grad_pass(
        images, info, closing, rows, own, ring_sums, s_u, s_ut, s_w, energy, lax.axis_size(DP)
    )
    return (loss.reshape(-1), sum_pass(exchange(grad, DP)))


def solution(mesh):
    parts = Mesh(mesh.devices.reshape(4, 4, 2, 4), ("z", "y", "c", "x"))
    return jax.shard_map(
        local,
        mesh=parts,
        in_specs=(P(DP, None), P(DP, None), P(DP, "x"), P(DP, "x"), P(DP), P(DP)),
        out_specs=(P(DP), P(DP, "x")),
        check_vma=False,
    )
```
